256 devices in a mesh: ctx: 32 (over x_lo, z, core), tp: 8 (over x_hi, y).
Axes of the slice: x: 4 (x_hi: 2, x_lo: 2; x = x_hi * 2 + x_lo), y: 4, z: 8, core: 2. Of those that a mesh axis runs over, the one named last changes fastest.
Arguments:
- prompt_x: bfloat16 [2048, 5120], P('ctx', 'tp'), may hold values from -6 to 6
- resp_x: bfloat16 [2048, 5120], P('ctx', 'tp'), may hold values from -6 to 6
- span_ids: int32 [64], replicated, may hold values from 0 to 63, each once
- lengths: int32 [16], replicated, may hold values from 16 to 128, as said below
- in_gain: float32 [5120], replicated, may hold values from 0.5 to 2
- q_gain: float32 [128], replicated, may hold values from 0.5 to 6, as said below
- k_gain: float32 [128], replicated, may hold values from 0.5 to 6, as said below
- w_query: bfloat16 [5120, 8192], P('ctx', 'tp'), may hold values from -0.078125 to 0.078125
- w_keyval: bfloat16 [5120, 2, 1024], P('ctx', None, 'tp'), may hold values from -0.078125 to 0.078125
- w_out: bfloat16 [8192, 5120], P('tp', 'ctx'), may hold values from -1 to 1
Outputs:
- prompt_out: bfloat16 [2048, 5120], P('ctx', 'tp')
- resp_out: bfloat16 [2048, 5120], P('ctx', 'tp')
The draws below stay inside these ranges and needn't reach their ends.
Inputs may be any that keep to these rules, and one draw needn't show every extreme that they name: `lengths`: one response has length 128 and one has 16. `q_gain`: positive. `k_gain`: positive.
All inputs are finite; a program needn't handle non-finite values.
Results may differ from the reference program's by a relative error of at most 0.02.
The reference program's roundings to bfloat16 on the way count: a program that leaves them out, or rounds other values in their place, can miss the bound.
Values may be sent and summed in bfloat16 or wider, within the bound.
A program may use at most 128 MiB of HBM per device.

```python
import math
import jax
import jax.numpy as jnp
from jax import lax

D = 5120
QH = 64
KVH = 8
HD = 128
PCH = 32
RLEN = 128
GROUP = 8
SPANS = 64
PROMPT = 2048
RESPONSES = 16


def spread_gain(key, low_end, high_end):
    uniform_draw = jax.random.uniform(key, (HD,), jnp.float32)
    return jnp.exp(jnp.log(low_end) + uniform_draw * (jnp.log(high_end) - jnp.log(low_end))).astype(jnp.float32)


def draw_q_gain(key, part):
    key = jax.random.fold_in(key, 11)
    return spread_gain(key, 0.5, 2.0)


def draw_k_gain(key, part):
    key = jax.random.fold_in(key, 13)
    return spread_gain(key, 0.5, 2.0)


def draw_lengths(key, part):
    key = jax.random.fold_in(key, 7)
    first_key, second_key = jax.random.split(key)
    drawn = jax.random.randint(first_key, (RESPONSES,), RLEN // 8, RLEN + 1)
    order = jax.random.permutation(second_key, RESPONSES)
    drawn = drawn.at[order[0]].set(RLEN).at[order[1]].set(RLEN // 8)
    return drawn.astype(jnp.int32)


def levels(rng, extent, cuts, smallest, high):
    level = 1.0
    for dim, blocks in cuts:
        draws = jax.random.uniform(jax.random.fold_in(jax.random.fold_in(rng, 6), dim), (blocks,), jnp.float32, smallest / len(cuts), high / len(cuts))
        level = level * jnp.repeat(jnp.exp(draws), extent[dim] // blocks).reshape((-1,) + (1,) * (len(extent) - 1 - dim))
    return level


def gaussian(key, shape, spread, limit, cuts=(), kind=jnp.bfloat16):
    values = spread * jax.random.normal(key, shape, jnp.float32)
    if cuts:
        values = values * levels(key, shape, cuts, -0.22, 0.18)
    return jnp.clip(values, -limit, limit).astype(kind)


def setup_inputs(seed: int = 0) -> dict:
    arg_keys = jax.random.split(jax.random.key(seed), 11)
    prompt_x = gaussian(arg_keys[0], (PROMPT, D), 1.0, 6.0, ((0, 32), (1, 8)))
    resp_x = gaussian(arg_keys[1], (RESPONSES * RLEN, D), 1.0, 6.0, ((0, 32), (1, 8)))
    span_ids = jax.random.permutation(arg_keys[2], SPANS).astype(jnp.int32)
    lengths = draw_lengths(jax.random.fold_in(arg_keys[10], 71), 0)
    in_gain = jnp.clip(jnp.exp(jax.random.uniform(arg_keys[4], (D,), jnp.float32, math.log(0.5), math.log(2.0))), 0.5, 2.0)
    q_gain = draw_q_gain(jax.random.fold_in(arg_keys[10], 71), 0)
    k_gain = draw_k_gain(jax.random.fold_in(arg_keys[10], 71), 0)
    w_query = gaussian(arg_keys[7], (D, QH * HD), D ** -0.5, 0.078125, ((0, 32), (1, 8)))
    w_keyval = gaussian(arg_keys[8], (D, 2, KVH * HD), D ** -0.5, 0.078125, ((0, 32), (2, 8)))
    w_out = gaussian(arg_keys[9], (QH * HD, D), (QH * HD // 256) ** -0.5, 1.0, ((0, 8), (1, 32)))
    return dict(prompt_x=prompt_x, resp_x=resp_x, span_ids=span_ids, lengths=lengths, in_gain=in_gain, q_gain=q_gain, k_gain=k_gain, w_query=w_query, w_keyval=w_keyval, w_out=w_out)


def head_norm(values, gain):
    return values * lax.rsqrt(lax.optimization_barrier(jnp.mean(values * values, axis=-1, keepdims=True)) + 1e-06) * gain

def rotary(values, positions):
    half_dim = values.shape[-1] // 2
    inverse = 1000000.0 ** (-(jnp.arange(half_dim, dtype=jnp.float32) * 2.0) / values.shape[-1])
    angles = positions.astype(jnp.float32)[:, None] * inverse[None, :]
    cosine = jnp.concatenate([jnp.cos(angles), jnp.cos(angles)], axis=-1)[:, None, :]
    sine = jnp.concatenate([jnp.sin(angles), jnp.sin(angles)], axis=-1)[:, None, :]
    rotated = jnp.concatenate([-values[..., half_dim:], values[..., :half_dim]], axis=-1)
    return values * cosine + rotated * sine

def attend(queries, keys, values, allowed):
    scores = jnp.einsum('qgd,kd->gqk', queries.astype(jnp.float32), keys.astype(jnp.float32)) * HD ** (-0.5)
    masked = jnp.where(allowed[None], scores, -1e+30)
    peak = lax.optimization_barrier(jnp.max(masked, axis=-1, keepdims=True))
    weights = jnp.where(allowed[None], jnp.exp(scores - peak), 0.0)
    total = lax.optimization_barrier(jnp.sum(weights, axis=-1))
    rounded = lax.optimization_barrier(weights.astype(jnp.bfloat16)).astype(jnp.float32)
    summed = jnp.einsum('gqk,kd->qgd', rounded, values.astype(jnp.float32))
    return summed / jnp.transpose(total)[:, :, None]

def reference(prompt_x, resp_x, span_ids, lengths, in_gain, q_gain, k_gain, w_query, w_keyval, w_out):
    total_rows = PROMPT + RESPONSES * RLEN
    joined = jnp.concatenate([prompt_x, resp_x], axis=0).astype(jnp.float32)
    normed = (joined * lax.rsqrt(lax.optimization_barrier(jnp.mean(joined * joined, axis=-1, keepdims=True)) + 1e-06) * in_gain).astype(jnp.bfloat16)
    query = jnp.dot(normed, w_query, preferred_element_type=jnp.float32)
    keyval = jnp.dot(normed, w_keyval.reshape(D, 2 * KVH * HD), preferred_element_type=jnp.float32)
    prompt_pos = (span_ids[:, None] * PCH + jnp.arange(PCH, dtype=jnp.int32)[None, :]).reshape(-1).astype(jnp.int32)
    resp_pos = (PROMPT + jnp.tile(jnp.arange(RLEN, dtype=jnp.int32), RESPONSES)).astype(jnp.int32)
    positions = jnp.concatenate([prompt_pos, resp_pos])
    queries = rotary(head_norm(query.reshape(total_rows, QH, HD), q_gain), positions).astype(jnp.bfloat16)
    queries = queries.reshape(total_rows, KVH, GROUP, HD)
    keys = rotary(head_norm(keyval[:, :KVH * HD].reshape(total_rows, KVH, HD), k_gain), positions).astype(jnp.bfloat16)
    values = keyval[:, KVH * HD:].reshape(total_rows, KVH, HD).astype(jnp.bfloat16)
    offsets = jnp.arange(RLEN, dtype=jnp.int32)
    causal = offsets[None, :] <= offsets[:, None]
    prompt_allowed = prompt_pos[None, :] <= prompt_pos[:, None]
    resp_allowed = jnp.concatenate([jnp.ones((RLEN, PROMPT), bool), causal], axis=1)

    def per_head(head):
        head_q = queries[:, head]
        head_k = keys[:, head]
        head_v = values[:, head]
        prompt_part = attend(head_q[:PROMPT], head_k[:PROMPT], head_v[:PROMPT], prompt_allowed)

        def per_resp(index):
            first = PROMPT + index * RLEN
            resp_q = lax.dynamic_slice_in_dim(head_q, first, RLEN, 0)
            resp_k = lax.dynamic_slice_in_dim(head_k, first, RLEN, 0)
            resp_v = lax.dynamic_slice_in_dim(head_v, first, RLEN, 0)
            return attend(resp_q, jnp.concatenate([head_k[:PROMPT], resp_k]), jnp.concatenate([head_v[:PROMPT], resp_v]), resp_allowed)
        resp_part = lax.map(per_resp, jnp.arange(RESPONSES, dtype=jnp.int32)).reshape(RESPONSES * RLEN, GROUP, HD)
        return jnp.concatenate([prompt_part, resp_part], axis=0)
    stacked = lax.map(per_head, jnp.arange(KVH, dtype=jnp.int32))
    attended = jnp.transpose(stacked, (1, 0, 2, 3)).reshape(total_rows, QH * HD).astype(jnp.bfloat16)
    projected = jnp.dot(attended, w_out, preferred_element_type=jnp.float32)
    keep_resp = (offsets[None, :] < lengths[:, None]).reshape(-1)
    keep = jnp.concatenate([jnp.ones((PROMPT,), bool), keep_resp])
    result = jnp.where(keep[:, None], projected, 0.0).astype(jnp.bfloat16)
    return (result[:PROMPT], result[PROMPT:])
```

```python
import functools

import jax
import jax.numpy as jnp
import numpy as np
from jax import lax
from jax.experimental import pallas as pl
from jax.experimental.pallas import tpu as pltpu
from jax.sharding import PartitionSpec as P

MESH = pl.DeviceIdType.MESH
BF = jnp.bfloat16
F32 = jnp.float32
NT = (((1,), (1,)), ((), ()))


def remote(src, dst, send, recv, dev):
    return pltpu.make_async_remote_copy(
        src_ref=src, dst_ref=dst, send_sem=send, recv_sem=recv, device_id=dev, device_id_type=MESH
    )


class Ring:
    def __init__(self, view, send, recv, z, up_dev, down_dev, parts=2):
        self.view, self.send, self.recv, self.z, self.parts = view, send, recv, z, parts
        self.devs = (up_dev, down_dev)

    def items(self, step):
        every = [(way, part) for part in range(self.parts) for way in (0, 1)]
        return every if step < 3 else [i for i in every if i[0] == i[1] * 2 // self.parts]

    def block(self, way, step):
        return lax.rem(self.z + (8 - step if way == 0 else step), 8)

    def copy(self, way, step, part, src=None):
        there = self.view(self.block(way, step), part)
        return remote(
            there if src is None else src, there,
            self.send.at[way, step, part], self.recv.at[way, step, part], self.devs[way],
        )

    def arrived(self, way, step, part):
        here = self.view(self.block(way, step + 1), part)
        remote(
            here, here, self.send.at[way, step, part], self.recv.at[way, step, part],
            self.devs[way],
        ).wait_recv()

    def start(self, part, src=None):
        for way in (0, 1):
            self.copy(way, 0, part, src).start()

    def forward(self, step, then=None, parts=None):
        for way, part in self.items(step - 1):
            if parts is not None and part not in parts:
                continue
            self.arrived(way, step - 1, part)
            if step < 4 and (way, part) in self.items(step):
                self.copy(way, step, part).start()
            if then is not None:
                then(way, step - 1, part)

    def last(self, then=None):
        self.forward(4, then)

    def drain(self):
        for step in range(4):
            for way, part in self.items(step):
                self.copy(way, step, part).wait_send()


class Plane:
    def __init__(self, view, src, a, b, a_dev, b_dev, sems):
        self.view, self.src, self.a, self.b = view, src, a, b
        self.a_dev, self.b_dev = a_dev, b_dev
        self.sa, self.ra, self.sb, self.rb = sems
        self.drains = []

    def go(self, src, dst, send, recv, to):
        make = lambda: remote(src, dst, send, recv, to)
        make().start()
        self.drains.append(lambda: make().wait_send())

    def wait(self, dst, recv, to):
        remote(dst, dst, recv, recv, to).wait_recv()

    def near(self, at, way):
        return (at + (1 if way == 0 else 3)) % 4

    def entry(self, j):
        at = [self.a, self.near(self.a, 1), self.near(self.a, 0)] + [(self.a + 2) % 4] * 2
        return at[j], (None if j < 3 else j - 3)

    def send_a(self):
        own = self.view(self.a, self.b)
        for way in (0, 1):
            self.go(
                self.src, own, self.sa.at[0, way], self.ra.at[0, way],
                self.a_dev(self.near(self.a, way)),
            )

    def send_b(self, j, src=None):
        at, half = self.entry(j)
        part = self.view(at, self.b, half)
        for way in (0, 1):
            self.go(
                part if src is None else src, part, self.sb.at[0, way, j], self.rb.at[0, way, j],
                self.b_dev(self.near(self.b, way)),
            )

    def pass_a(self):
        for way in (0, 1):
            at = self.near(self.a, 1 - way)
            self.wait(self.view(at, self.b), self.ra.at[0, way], self.a_dev(at))
            half = self.view(at, self.b, way)
            self.go(
                half, half, self.sa.at[1, way], self.ra.at[1, way],
                self.a_dev(self.near(self.a, way)),
            )
            self.send_b(1 + way)

    def pass_far(self):
        far = (self.a + 2) % 4
        for way in (0, 1):
            self.wait(self.view(far, self.b, way), self.ra.at[1, way], self.a_dev(far))
            self.send_b(3 + way)

    def pass_b(self, j):
        at, half = self.entry(j)
        for way in (0, 1):
            near = self.near(self.b, 1 - way)
            self.wait(self.view(at, near, half), self.rb.at[0, way, j], self.b_dev(near))
            if half is None or half == way:
                part = self.view(at, near, way)
                self.go(
                    part, part, self.sb.at[1, way, j], self.rb.at[1, way, j],
                    self.b_dev(self.near(self.b, way)),
                )

    def end_b(self, j):
        at, half = self.entry(j)
        far = (self.b + 2) % 4
        for way in (0, 1):
            if half is None or half == way:
                self.wait(self.view(at, far, way), self.rb.at[1, way, j], self.b_dev(far))


class Spread:
    def __init__(self, view, other, sems, z, to_z, twin):
        self.view, self.other, self.z, self.to_z, self.twin = view, other, z, to_z, twin
        self.send, self.recv, self.tsend, self.trecv = sems

    def make(self, way, k, sender):
        sign = 1 if way == 0 else -1
        hops, owner = ((1, 0), (2, 0), (1, 2), (2, 2))[k]
        start = self.z if sender else self.z - sign * hops
        block = (start - sign * owner + 16) % 8
        part = self.view(block, way if k == 3 else None)
        return remote(
            part, part, self.send.at[way, k], self.recv.at[way, k],
            self.to_z((self.z + sign * hops + 8) % 8),
        )

    def pair(self, way, k, view):
        sign = 1 if way == 0 else -1
        block = (self.z - sign * (k + 1) + 16) % 8
        part = view(block, way if k == 3 else None)
        return remote(part, part, self.tsend.at[way, k], self.trecv.at[way, k], self.twin)

    def start(self):
        for k in (1, 0):
            for way in (0, 1):
                self.make(way, k, True).start()

    def arrive(self, way, k):
        self.make(way, k, False).wait_recv()
        self.pair(way, k, self.view).start()

    def middle(self):
        for way in (0, 1):
            self.arrive(way, 1)
            self.make(way, 3, True).start()
            self.make(way, 2, True).start()
        for way in (0, 1):
            self.arrive(way, 0)

    def last(self):
        for k in (3, 2):
            for way in (0, 1):
                self.arrive(way, k)

    def twins(self):
        for k in range(4):
            for way in (0, 1):
                self.pair(way, k, self.other).wait_recv()

    def drain(self):
        for k in range(4):
            for way in (0, 1):
                self.make(way, k, True).wait_send()
                self.pair(way, k, self.view).wait_send()


class Plane:
    def __init__(self, view, src, a, b, a_dev, b_dev, sems):
        self.view, self.src, self.a, self.b = view, src, a, b
        self.a_dev, self.b_dev = a_dev, b_dev
        self.sa, self.ra, self.sb, self.rb = sems
        self.drains = []

    def go(self, src, dst, send, recv, to):
        make = lambda: remote(src, dst, send, recv, to)
        make().start()
        self.drains.append(lambda: make().wait_send())

    def wait(self, dst, recv, to):
        remote(dst, dst, recv, recv, to).wait_recv()

    def near(self, at, way):
        return (at + (1 if way == 0 else 3)) % 4

    def entry(self, j):
        at = [self.a, self.near(self.a, 1), self.near(self.a, 0)] + [(self.a + 2) % 4] * 2
        return at[j], (None if j < 3 else j - 3)

    def send_a(self):
        own = self.view(self.a, self.b)
        for way in (0, 1):
            self.go(
                self.src, own, self.sa.at[0, way], self.ra.at[0, way],
                self.a_dev(self.near(self.a, way)),
            )

    def send_b(self, j, src=None):
        at, half = self.entry(j)
        part = self.view(at, self.b, half)
        for way in (0, 1):
            self.go(
                part if src is None else src, part, self.sb.at[0, way, j], self.rb.at[0, way, j],
                self.b_dev(self.near(self.b, way)),
            )

    def pass_a(self):
        for way in (0, 1):
            at = self.near(self.a, 1 - way)
            self.wait(self.view(at, self.b), self.ra.at[0, way], self.a_dev(at))
            half = self.view(at, self.b, way)
            self.go(
                half, half, self.sa.at[1, way], self.ra.at[1, way],
                self.a_dev(self.near(self.a, way)),
            )
            self.send_b(1 + way)

    def pass_far(self):
        far = (self.a + 2) % 4
        for way in (0, 1):
            self.wait(self.view(far, self.b, way), self.ra.at[1, way], self.a_dev(far))
            self.send_b(3 + way)

    def pass_b(self, j):
        at, half = self.entry(j)
        for way in (0, 1):
            near = self.near(self.b, 1 - way)
            self.wait(self.view(at, near, half), self.rb.at[0, way, j], self.b_dev(near))
            if half is None or half == way:
                part = self.view(at, near, way)
                self.go(
                    part, part, self.sb.at[1, way, j], self.rb.at[1, way, j],
                    self.b_dev(self.near(self.b, way)),
                )

    def end_b(self, j):
        at, half = self.entry(j)
        far = (self.b + 2) % 4
        for way in (0, 1):
            if half is None or half == way:
                self.wait(self.view(at, far, way), self.rb.at[1, way, j], self.b_dev(far))


class Twin:
    def __init__(self, ring, other, send, recv, dev):
        self.ring, self.other, self.sems, self.dev = ring, other, (send, recv), dev

    def make(self, way, step, half, view):
        part = view(self.ring.block(way, step + 1), half)
        return remote(
            part, part, self.sems[0].at[way, step, half], self.sems[1].at[way, step, half], self.dev
        )

    def __call__(self, way, step, half):
        self.make(way, step, half, self.ring.view).start()

    def each(self, steps):
        return [(way, step, half) for step in steps for way, half in self.ring.items(step)]

    def wait_recv(self, steps):
        for item in self.each(steps):
            self.make(*item, self.other).wait_recv()

    def drain(self):
        for item in self.each(range(4)):
            self.make(*item, self.ring.view).wait_send()


def rows_of(start, size, unit):
    return pl.ds(pl.multiple_of(start, unit), size)


def kernel(
    spans, lens, px, rx, gain, qg, kg, inv, wq, wkv, wo,
    po, ro,
    xr, nb, wqb, wkb, wob, wkl, accq, acck, cosb, sinb, rpos, kpos, qb, kvp, kvr, atts, attb,
    osend, ry, xs, xrx,
    loc, xas, xar, xbs, xbr, gs, gr, ks, kr, qrs, qrr, krs, krr, ors, orr, ots, otr, o1,
    nbs, nbr, kvs, kvrv, vrs, vrr, vts, vtr, ats, atr, ys, yr, zs, zr,
):
    ctx, tp = lax.axis_index("ctx"), lax.axis_index("tp")
    low, z, c = ctx // 16, (ctx // 2) % 8, ctx % 2
    hi, y = tp // 4, tp % 4
    x = hi * 2 + low
    olow, oc = 1 - low, 1 - c

    def dev(low_, z_, c_, hi_, y_):
        return (low_ * 16 + z_ * 2 + c_, hi_ * 4 + y_)

    def at_x(x_):
        return dev(x_ % 2, z, c, x_ // 2, y)

    def at_y(y_):
        return dev(low, z, c, hi, y_)

    def at_g(low_, c_):
        return dev(low_, z, c_, hi, y)

    x_up, x_dn, x_far = (x + 1) % 4, (x + 3) % 4, (x + 2) % 4
    y_up, y_dn, y_far = (y + 1) % 4, (y + 3) % 4, (y + 2) % 4
    z_up = dev(low, (z + 1) % 8, c, hi, y)
    z_dn = dev(low, (z + 7) % 8, c, hi, y)
    twin = at_g(low, oc)
    group = [(low, oc), (olow, c), (olow, oc)]

    partners = [at_g(*m) for m in group] + [z_up, z_dn]
    partners += [at_y(y_up), at_y(y_dn), at_y(y_far)]
    partners += [dev(low, (z + 2) % 8, c, hi, y), dev(low, (z + 6) % 8, c, hi, y)]
    partners += [dev(low, z, c, 1 - hi, y), dev(olow, z, c, 1 - hi, y)]
    barrier = pltpu.get_barrier_semaphore()
    for partner in partners:
        pl.semaphore_signal(barrier, inc=1, device_id=partner, device_id_type=MESH)
    for kind in range(2):
        wkl[kind] = wkv[:, kind, :]
    pl.semaphore_wait(barrier, len(partners))

    drains = []

    def finish():
        for drain in drains:
            drain()

    def block_of(part, x_, y_, half=None):
        first, count = (0, 64) if half is None else (half * 32, 32)
        return xr.at[
            part, rows_of((x_ % 2) * 64 + first, count, 32),
            rows_of(((x_ // 2) * 4 + y_) * 640, 640, 128),
        ]

    prompts = Plane(
        lambda a, b, h=None: block_of(0, a, b, h), px, x, y, at_x, at_y,
        (xas.at[0], xar.at[0], xbs.at[0], xbr.at[0]),
    )
    answers = Plane(
        lambda a, b, h=None: block_of(1, b, a, h), rx, y, x, at_y, at_x,
        (xas.at[1], xar.at[1], xbs.at[1], xbr.at[1]),
    )
    planes = (prompts, answers)
    own0, own1 = block_of(0, x, y), block_of(1, x, y)

    group4 = [(low, c)] + group

    def piece(buf, z_, low_, c_):
        return buf.at[rows_of(low_ * 2560 + z_ * 320 + c_ * 160, 160, 32)]

    def wq_cols(low_, c_):
        return wq.at[:, rows_of((low_ * 2 + c_) * 256, 256, 256)]

    def wq_send(i):
        low_, c_ = group[i]
        return remote(
            wq_cols(low_, c_), piece(wqb, z, low, c), gs.at[i], gr.at[i], at_g(low_, c_)
        )

    def wk_cols(low_):
        return wkl.at[low_]

    def wk_send(i, low_):
        return remote(wk_cols(low_), piece(wkb, z, low, c), ks.at[i], kr.at[i], at_g(low_, 0))

    qring = Ring(
        lambda z_, p: piece(wqb, z_, *group4[p]), qrs, qrr, z, z_up, z_dn, 4
    )
    kring = Ring(
        lambda z_, p: piece(wkb, z_, *group4[p]), krs, krr, z, z_up, z_dn, 4
    )

    def if_keys(run):
        pl.when(c == 0)(run)

    prompts.send_a()
    prompts.send_b(0, px)

    @pl.when(c == 0)
    def _():
        kring.start(0, wk_cols(low))
        wk_send(1, olow).start()
        pltpu.make_async_copy(wk_cols(low), piece(wkb, z, low, c), loc.at[3]).start()

    @pl.when(c == 1)
    def _():
        wk_send(0, low).start()
        wk_send(2, olow).start()

    for i in range(3):
        wq_send(i).start()
    qring.start(0, wq_cols(low, c))
    answers.send_a()
    answers.send_b(0, rx)

    local0 = pltpu.make_async_copy(px, own0, loc.at[0])
    local1 = pltpu.make_async_copy(rx, own1, loc.at[1])
    local2 = pltpu.make_async_copy(wq_cols(low, c), piece(wqb, z, low, c), loc.at[2])
    local0.start()
    local1.start()
    local2.start()

    def wo_view(c_):
        return lambda z_, h: wob.at[rows_of(z_ * 320 + c_ * 160 + h * 80, 80, 16)]

    wo_own = wob.at[rows_of(z * 320 + c * 160, 160, 32)]
    local4 = pltpu.make_async_copy(wo, wo_own, loc.at[4])
    local4.start()

    oring = Ring(wo_view(c), ors, orr, z, z_up, z_dn)
    otwin = Twin(oring, wo_view(oc), ots, otr, twin)
    for h in range(2):
        oring.start(h, wo.at[pl.ds(h * 80, 80)])
    remote(wo, wo_own, o1.at[0], o1.at[1], twin).start()
    drains.append(lambda: remote(wo_own, wo_own, o1.at[0], o1.at[1], twin).wait_send())
    drains.append(oring.drain)
    drains.append(otwin.drain)

    @if_keys
    def _():
        for i in range(3):
            here = piece(wkb, z, *group[i])
            remote(here, here, ks.at[i], kr.at[i], twin).wait_recv()
            kring.start(i + 1)

    prompts.pass_a()
    prompts.pass_b(0)
    for i in range(3):
        here = piece(wqb, z, *group[i])
        remote(here, here, gs.at[i], gr.at[i], twin).wait_recv()
        qring.start(i + 1)
    prompts.pass_far()
    if_keys(lambda: kring.forward(1))
    answers.pass_a()
    qring.forward(1, parts=(0,))
    prompts.pass_b(1)
    prompts.pass_b(2)
    if_keys(lambda: kring.forward(2))
    prompts.pass_b(3)
    prompts.pass_b(4)
    answers.pass_b(0)
    answers.pass_far()
    qring.forward(1, parts=(1, 2, 3))
    if_keys(lambda: kring.forward(3))

    iota = lax.broadcasted_iota(jnp.int32, (32, 128), 0)
    for c_ in range(2):
        for low_ in range(2):
            for h in range(2):
                sid = spans[2 * (low_ * 16 + z * 2 + c_) + h]
                first = c_ * 128 + low_ * 64 + h * 32
                rpos[pl.ds(first, 32), :] = (sid * 32 + iota).astype(F32)
                rpos[pl.ds(256 + first, 32), :] = (2048 + c_ * 64 + h * 32 + iota).astype(F32)
    first_half = lax.broadcasted_iota(jnp.int32, (128, 128), 1) < 64

    @pl.loop(0, 4)
    def _(i):
        rows = rows_of(i * 128, 128, 128)
        angles = rpos[rows, :] * inv[...]
        cosb[rows, :] = jnp.cos(angles)
        sine = jnp.sin(angles)
        sinb[rows, :] = jnp.where(first_half, -sine, sine)

    for copy in (local0, local1, local2, local4):
        copy.wait()
    for j in range(5):
        prompts.end_b(j)

    drains.append(lambda: [drain() for plane in planes for drain in plane.drains])
    drains.append(qring.drain)
    drains.append(lambda: [wq_send(i).wait_send() for i in range(3)])

    def drain_keys():
        @pl.when(c == 0)
        def _():
            kring.drain()
            wk_send(1, olow).wait_send()

        @pl.when(c == 1)
        def _():
            wk_send(0, low).wait_send()
            wk_send(2, olow).wait_send()

    drains.append(drain_keys)

    def normed(c_, g):
        return nb.at[rows_of((g // 2) * 256 + c_ * 128 + (g % 2) * 64, 64, 64)]

    def norm_send(c_, g):
        return remote(normed(c_, g), normed(c_, g), nbs.at[g], nbr.at[g], twin)

    def norm(g):
        @pl.loop(0, 4)
        def _(i):
            rows = xr[g // 2, rows_of((g % 2) * 64 + i * 16, 16, 16), :].astype(F32)
            mean = jnp.mean(rows * rows, axis=-1, keepdims=True)
            first = (g // 2) * 256 + c * 128 + (g % 2) * 64 + i * 16
            nb[rows_of(first, 16, 16), :] = (
                rows * lax.rsqrt(mean + 1e-06) * gain[...]
            ).astype(BF)

        norm_send(c, g).start()

    drains.append(lambda: [norm_send(c, g).wait_send() for g in range(4)])
    norm(0)
    norm(1)
    if_keys(kring.last)
    if_keys(lambda: pltpu.make_async_copy(wk_cols(low), piece(wkb, z, low, c), loc.at[3]).wait())
    qring.forward(2, parts=(0,))
    for j in range(1, 5):
        answers.pass_b(j)
    for g in range(2):
        norm_send(oc, g).wait_recv()

    def head(values, gains, rows):
        mean = jnp.mean(values * values, axis=-1, keepdims=True)
        values = values * lax.rsqrt(mean + 1e-06) * gains[...]
        return values * cosb[rows, :] + pltpu.roll(values, 64, 1) * sinb[rows, :]

    def kv_send(i, p):
        low_, c_ = group[i]
        own = kvp.at[low, rows_of(z * 256, 256, 256)] if p == 0 else kvr.at[low]
        return remote(
            own, own, kvs.at[i, p], kvrv.at[0 if i == 0 else 1, p], at_g(low_, c_)
        )

    def keys(p):
        rows = pl.ds(p * 256, 256)
        acck[rows, :] = jnp.zeros((256, 128), F32)

        @pl.loop(0, 10)
        def _(i):
            part = rows_of(i * 512, 512, 512)
            acck[rows, :] += jnp.dot(nb[rows, part], wkb[part, :], preferred_element_type=F32)

        raw = acck[rows, :]
        mine = jnp.where(low == 0, head(raw, kg, rows), raw).astype(BF)
        if p == 0:
            kvp[low, rows_of(z * 256, 256, 256), :] = mine
        else:
            kvr[low] = mine
        for k in (1, 2, 0):
            kv_send(k, p).start()

    if_keys(lambda: keys(0))
    qring.forward(2, parts=(1, 2, 3))
    for j in range(5):
        answers.end_b(j)
    norm(2)
    norm(3)

    def drain_kv():
        @pl.when(c == 0)
        def _():
            for p in range(2):
                for i in range(3):
                    kv_send(i, p).wait_send()

    drains.append(drain_kv)

    def kv_wait(kind, i, p):
        part = kvp.at[kind, rows_of(z * 256, 256, 256)] if p == 0 else kvr.at[kind]
        remote(part, part, kvs.at[0, p], kvrv.at[i, p], twin).wait_recv()

    lane = lax.broadcasted_iota(jnp.int32, (8, 2048), 1)

    def key_positions(j, held):
        z_, c_, low_, h = j // 8, (j // 4) % 2, (j // 2) % 2, j % 2
        sid = spans[2 * (low_ * 16 + z_ * 2 + c_) + h]
        return jnp.where(lane // 32 == j, sid * 32 + lane % 32, held)

    kpos[...] = lax.fori_loop(
        0, 64, key_positions, jnp.zeros((8, 2048), jnp.int32)
    ).astype(F32)
    pl.when(c == 1)(lambda: kv_wait(low, 0, 0))
    kv_wait(olow, 1, 0)

    def kv_view(kind):
        def view(z_, h):
            first, count = (0, 256) if h is None else (h * 128, 128)
            return kvp.at[kind, rows_of(z_ * 256 + first, count, 128)]

        return view

    spread = Spread(
        kv_view(c), kv_view(oc), (vrs, vrr, vts, vtr), z,
        lambda z_: dev(low, z_, c, hi, y), twin,
    )
    spread.start()
    drains.append(spread.drain)
    qring.forward(3)
    oring.forward(1, otwin, (0,))
    for g in (2, 3):
        norm_send(oc, g).wait_recv()
    spread.middle()
    if_keys(lambda: keys(1))
    oring.forward(1, otwin, (1,))
    qring.last()
    accq[...] = jnp.zeros_like(accq)

    @pl.loop(0, 10)
    def _(i):
        part = rows_of(i * 512, 512, 512)
        accq[...] += jnp.dot(nb[:, part], wqb[part, :], preferred_element_type=F32)

    spread.last()
    for i in range(4):
        rows = pl.ds(i * 128, 128)
        for h in range(2):
            qb[i, pl.ds(h * 128, 128), :] = head(
                accq[rows, pl.ds(h * 128, 128)], qg, rows
            ).astype(BF)
    oring.forward(2, otwin)
    pl.when(c == 1)(lambda: kv_wait(low, 0, 1))
    kv_wait(olow, 1, 1)
    spread.twins()

    scale = 128 ** (-0.5)

    def attend(c_, p):
        queries = qb[p * 2 + c_]
        scores = lax.dot_general(queries, kvp[0], NT, preferred_element_type=F32) * scale
        if p == 0:
            mine = rpos[rows_of(c_ * 128, 128, 128), :][:, :1]
            allowed = kpos[:1, :] <= jnp.concatenate([mine, mine], axis=0)
            scores = jnp.where(allowed, scores, -1e30)
        peak = jnp.max(scores, axis=-1, keepdims=True)
        if p == 1:
            own = lax.dot_general(queries, kvr[0], NT, preferred_element_type=F32) * scale
            q_row = lax.broadcasted_iota(jnp.int32, (256, 256), 0) % 128
            k_row = lax.broadcasted_iota(jnp.int32, (256, 256), 1)
            allowed = ((q_row // 64) == ((k_row // 64) % 2)) & (
                (k_row // 128) * 64 + k_row % 64 <= c_ * 64 + q_row % 64
            )
            own = jnp.where(allowed, own, -1e30)
            peak = jnp.maximum(peak, jnp.max(own, axis=-1, keepdims=True))
        weights = jnp.exp(scores - peak)
        total = jnp.sum(weights, axis=-1, keepdims=True)
        summed = jnp.dot(weights.astype(BF), kvp[1], preferred_element_type=F32)
        if p == 1:
            more = jnp.exp(own - peak)
            total = total + jnp.sum(more, axis=-1, keepdims=True)
            summed = summed + jnp.dot(more.astype(BF), kvr[1], preferred_element_type=F32)
        result = (summed / total).astype(BF)
        for h in range(2):
            atts[c_, pl.ds(p * 128, 128), pl.ds(h * 128, 128)] = result[h * 128 : (h + 1) * 128]

    def att_cols(low_, c_):
        return attb.at[:, rows_of((low_ * 2 + c_) * 256, 256, 256)]

    def att_send(i):
        low_, c_ = group[i]
        return remote(atts.at[c_], att_cols(low, c), ats.at[i], atr.at[i], at_g(low_, c_))

    attend(oc, 0)
    attend(oc, 1)
    att_send(2).start()
    att_send(0).start()
    attend(c, 0)
    attend(c, 1)
    att_send(1).start()
    drains.append(lambda: [att_send(i).wait_send() for i in range(3)])
    attb[:, rows_of((low * 2 + c) * 256, 256, 256)] = atts[c]
    other_own = wob.at[rows_of(z * 320 + oc * 160, 160, 32)]
    remote(other_own, other_own, o1.at[0], o1.at[1], twin).wait_recv()
    otwin.wait_recv(range(2))
    for i in range(3):
        part = att_cols(*group[i])
        remote(part, part, ats.at[i], atr.at[i], twin).wait_recv()

    def y_send(k, p, y_):
        place = (y_ - y + 3) % 4
        rows = pl.ds(p * 128, 128)
        return remote(
            osend.at[k, rows], ry.at[place, rows], ys.at[k, p], yr.at[place, p], at_y(y_)
        )

    def y_of(k):
        return (z // 2 + (0, 3 + 2 * (z % 2), 5 - 2 * (z % 2), 2)[k]) % 4

    def project(k):
        y_ = y_of(k)
        weights = wob[rows_of(y_ * 640, 640, 128), :]
        for p in range(2):
            rows = pl.ds(p * 128, 128)
            osend[k, rows, :] = lax.dot_general(
                attb[rows, :], weights, NT, preferred_element_type=F32
            ).astype(BF)
            pl.when(y_ != y)(lambda: y_send(k, p, y_).start())

    def drain_y():
        for k in range(4):
            for p in range(2):
                pl.when(y_of(k) != y)(lambda k=k, p=p: y_send(k, p, y_of(k)).wait_send())

    drains.append(drain_y)
    project(0)
    project(1)
    oring.forward(3, otwin)
    otwin.wait_recv((2,))
    project(2)
    oring.last(otwin)
    otwin.wait_recv((3,))
    project(3)

    def x_send(low_, p):
        return remote(
            xs.at[pl.ds(p * 128 + low_ * 64, 64)], xrx.at[hi, p],
            zs.at[low_, p], zr.at[hi, p], dev(low_, z, c, low, y),
        )

    mine = (y - z // 2 + 4) % 4
    slot = jnp.where(mine == 2, 3, jnp.where(mine % 2 == 0, 0, 2 - (mine // 2 + z) % 2))
    for p in range(2):
        rows = pl.ds(p * 128, 128)
        total = osend[slot, rows, :].astype(F32)
        for i in range(3):
            part = ry.at[i, rows]
            remote(part, part, ys.at[0, p], yr.at[i, p], twin).wait_recv()
            total += ry[i, rows, :].astype(F32)
        xs[rows, :] = total.astype(BF)
        for low_ in range(2):
            here = jnp.logical_and(hi == low, low == low_)

            @pl.when(here)
            def _(low_=low_, p=p):
                xrx[hi, p] = xs[pl.ds(p * 128 + low_ * 64, 64), :]

            pl.when(jnp.logical_not(here))(lambda low_=low_, p=p: x_send(low_, p).start())

    offsets = c * 64 + lax.broadcasted_iota(jnp.int32, (64, 640), 0)
    for p in range(2):
        for hi_ in range(2):

            @pl.when(jnp.logical_not(jnp.logical_and(hi == low, hi == hi_)))
            def _(hi_=hi_, p=p):
                part = xrx.at[hi_, p]
                remote(part, part, zs.at[0, p], zr.at[hi_, p], twin).wait_recv()

        total = xrx[0, p].astype(F32) + xrx[1, p].astype(F32)
        if p == 0:
            po[...] = total.astype(BF)
        else:
            ro[...] = jnp.where(offsets < lens[ctx // 2], total, 0.0).astype(BF)

    finish()
    for low_ in range(2):
        here = jnp.logical_and(hi == low, low == low_)

        @pl.when(jnp.logical_not(here))
        def _(low_=low_):
            for p in range(2):
                x_send(low_, p).wait_send()


def body(prompt_x, resp_x, span_ids, lengths, in_gain, q_gain, k_gain, w_query, w_keyval, w_out):
    half = 1000000.0 ** (-(np.arange(64) * 2.0) / 128)
    inverse = np.concatenate([half, half])[None, :].astype(np.float32)
    dma = pltpu.SemaphoreType.DMA
    hbm, vmem, smem = (pl.BlockSpec(memory_space=s) for s in (pl.ANY, pltpu.VMEM, pltpu.SMEM))
    out = jax.ShapeDtypeStruct((64, 640), BF)
    return pl.pallas_call(
        kernel,
        out_shape=(out, out),
        in_specs=[smem, smem, hbm, hbm, vmem, vmem, vmem, vmem, hbm, vmem, hbm],
        out_specs=(vmem, vmem),
        scratch_shapes=[
            pltpu.VMEM((2, 128, 5120), BF),
            pltpu.VMEM((512, 5120), BF),
            pltpu.VMEM((5120, 256), BF),
            pltpu.VMEM((5120, 128), BF),
            pltpu.VMEM((2560, 1024), BF),
            pltpu.VMEM((2, 160, 128), BF),
            pltpu.VMEM((512, 256), F32),
            pltpu.VMEM((512, 128), F32),
            pltpu.VMEM((512, 128), F32),
            pltpu.VMEM((512, 128), F32),
            pltpu.VMEM((512, 128), F32),
            pltpu.VMEM((8, 2048), F32),
            pltpu.VMEM((4, 256, 128), BF),
            pltpu.VMEM((2, 2048, 128), BF),
            pltpu.VMEM((2, 256, 128), BF),
            pltpu.VMEM((2, 256, 256), BF),
            pltpu.VMEM((256, 1024), BF),
            pltpu.VMEM((4, 256, 640), BF),
            pltpu.VMEM((3, 256, 640), BF),
            pltpu.VMEM((256, 640), BF),
            pltpu.VMEM((2, 2, 64, 640), BF),
            dma((5,)),
            dma((2, 2, 2)), dma((2, 2, 2)),
            dma((2, 2, 2, 5)), dma((2, 2, 2, 5)),
            dma((3,)), dma((3,)),
            dma((3,)), dma((3,)),
            dma((2, 4, 4)), dma((2, 4, 4)),
            dma((2, 4, 4)), dma((2, 4, 4)),
            dma((2, 4, 2)), dma((2, 4, 2)),
            dma((2, 4, 2)), dma((2, 4, 2)),
            dma((2,)),
            dma((4,)), dma((4,)),
            dma((3, 2)), dma((2, 2)),
            dma((2, 4)), dma((2, 4)),
            dma((2, 4)), dma((2, 4)),
            dma((3,)), dma((3,)),
            dma((4, 2)), dma((3, 2)),
            dma((2, 2)), dma((2, 2)),
        ],
        compiler_params=pltpu.CompilerParams(
            collective_id=0, has_side_effects=True, vmem_limit_bytes=56 * 2**20
        ),
        name="attention_block",
    )(
        span_ids, lengths, prompt_x, resp_x, in_gain[None, :], q_gain[None, :], k_gain[None, :],
        inverse, w_query, w_keyval, jnp.transpose(w_out),
    )


def solution(mesh):
    placed = (
        P("ctx", "tp"),
        P("ctx", "tp"),
        P(),
        P(),
        P(),
        P(),
        P(),
        P("ctx", "tp"),
        P("ctx", None, "tp"),
        P("tp", "ctx"),
    )
    return jax.shard_map(
        body,
        mesh=mesh,
        in_specs=placed,
        out_specs=(P("ctx", "tp"), P("ctx", "tp")),
        check_vma=False,
    )
```

```python
import functools

import jax
import jax.numpy as jnp
import numpy as np
from jax import lax
from jax.experimental import pallas as pl
from jax.experimental.pallas import tpu as pltpu
from jax.sharding import PartitionSpec as P

MESH = pl.DeviceIdType.MESH
BF = jnp.bfloat16
F32 = jnp.float32
NT = (((1,), (1,)), ((), ()))


def remote(src, dst, send, recv, dev):
    return pltpu.make_async_remote_copy(
        src_ref=src, dst_ref=dst, send_sem=send, recv_sem=recv, device_id=dev, device_id_type=MESH
    )


class Ring:
    def __init__(self, view, send, recv, z, up_dev, down_dev, parts=2):
        self.view, self.send, self.recv, self.z, self.parts = view, send, recv, z, parts
        self.devs = (up_dev, down_dev)

    def items(self, step):
        every = [(way, part) for part in range(self.parts) for way in (0, 1)]
        return every if step < 3 else [i for i in every if i[0] == i[1] * 2 // self.parts]

    def block(self, way, step):
        return lax.rem(self.z + (8 - step if way == 0 else step), 8)

    def copy(self, way, step, part, src=None):
        there = self.view(self.block(way, step), part)
        return remote(
            there if src is None else src, there,
            self.send.at[way, step, part], self.recv.at[way, step, part], self.devs[way],
        )

    def arrived(self, way, step, part):
        here = self.view(self.block(way, step + 1), part)
        remote(
            here, here, self.send.at[way, step, part], self.recv.at[way, step, part],
            self.devs[way],
        ).wait_recv()

    def start(self, part, src=None):
        for way in (0, 1):
            self.copy(way, 0, part, src).start()

    def forward(self, step, then=None, parts=None):
        for way, part in self.items(step - 1):
            if parts is not None and part not in parts:
                continue
            self.arrived(way, step - 1, part)
            if step < 4 and (way, part) in self.items(step):
                self.copy(way, step, part).start()
            if then is not None:
                then(way, step - 1, part)

    def last(self, then=None):
        self.forward(4, then)

    def drain(self):
        for step in range(4):
            for way, part in self.items(step):
                self.copy(way, step, part).wait_send()


class Plane:
    def __init__(self, view, src, a, b, a_dev, b_dev, sems):
        self.view, self.src, self.a, self.b = view, src, a, b
        self.a_dev, self.b_dev = a_dev, b_dev
        self.sa, self.ra, self.sb, self.rb = sems
        self.drains = []

    def go(self, src, dst, send, recv, to):
        make = lambda: remote(src, dst, send, recv, to)
        make().start()
        self.drains.append(lambda: make().wait_send())

    def wait(self, dst, recv, to):
        remote(dst, dst, recv, recv, to).wait_recv()

    def near(self, at, way):
        return (at + (1 if way == 0 else 3)) % 4

    def entry(self, j):
        at = [self.a, self.near(self.a, 1), self.near(self.a, 0)] + [(self.a + 2) % 4] * 2
        return at[j], (None if j < 3 else j - 3)

    def send_a(self):
        own = self.view(self.a, self.b)
        for way in (0, 1):
            self.go(
                self.src, own, self.sa.at[0, way], self.ra.at[0, way],
                self.a_dev(self.near(self.a, way)),
            )

    def send_b(self, j, src=None):
        at, half = self.entry(j)
        part = self.view(at, self.b, half)
        for way in (0, 1):
            self.go(
                part if src is None else src, part, self.sb.at[0, way, j], self.rb.at[0, way, j],
                self.b_dev(self.near(self.b, way)),
            )

    def pass_a(self):
        for way in (0, 1):
            at = self.near(self.a, 1 - way)
            self.wait(self.view(at, self.b), self.ra.at[0, way], self.a_dev(at))
            half = self.view(at, self.b, way)
            self.go(
                half, half, self.sa.at[1, way], self.ra.at[1, way],
                self.a_dev(self.near(self.a, way)),
            )
            self.send_b(1 + way)

    def pass_far(self):
        far = (self.a + 2) % 4
        for way in (0, 1):
            self.wait(self.view(far, self.b, way), self.ra.at[1, way], self.a_dev(far))
            self.send_b(3 + way)

    def pass_b(self, j):
        at, half = self.entry(j)
        for way in (0, 1):
            near = self.near(self.b, 1 - way)
            self.wait(self.view(at, near, half), self.rb.at[0, way, j], self.b_dev(near))
            if half is None or half == way:
                part = self.view(at, near, way)
                self.go(
                    part, part, self.sb.at[1, way, j], self.rb.at[1, way, j],
                    self.b_dev(self.near(self.b, way)),
                )

    def end_b(self, j):
        at, half = self.entry(j)
        far = (self.b + 2) % 4
        for way in (0, 1):
            if half is None or half == way:
                self.wait(self.view(at, far, way), self.rb.at[1, way, j], self.b_dev(far))


class Spread:
    def __init__(self, view, others, sems, z, to_z, devs):
        self.view, self.others, self.z, self.to_z, self.devs = view, others, z, to_z, devs
        self.send, self.recv, self.tsend, self.trecv = sems

    def make(self, way, k, sender):
        sign = 1 if way == 0 else -1
        hops, owner = ((1, 0), (2, 0), (1, 2), (2, 2))[k]
        start = self.z if sender else self.z - sign * hops
        block = (start - sign * owner + 16) % 8
        part = self.view(block, way if k == 3 else None)
        return remote(
            part, part, self.send.at[way, k], self.recv.at[way, k],
            self.to_z((self.z + sign * hops + 8) % 8),
        )

    def pair(self, way, k, i, view):
        sign = 1 if way == 0 else -1
        block = (self.z - sign * (k + 1) + 16) % 8
        part = view(block, way if k == 3 else None)
        return remote(
            part, part, self.tsend.at[i, way, k], self.trecv.at[i, way, k], self.devs[i]
        )

    def start(self):
        for k in (1, 0):
            for way in (0, 1):
                self.make(way, k, True).start()

    def arrive(self, way, k):
        self.make(way, k, False).wait_recv()
        for i in (1, 2, 0):
            self.pair(way, k, i, self.view).start()

    def middle(self):
        for way in (0, 1):
            self.arrive(way, 1)
            self.make(way, 3, True).start()
            self.make(way, 2, True).start()
        for way in (0, 1):
            self.arrive(way, 0)

    def last(self):
        for k in (3, 2):
            for way in (0, 1):
                self.arrive(way, k)

    def twins(self):
        for k in range(4):
            for way in (0, 1):
                for i in range(3):
                    self.pair(way, k, i, self.others[i]).wait_recv()

    def drain(self):
        for k in range(4):
            for way in (0, 1):
                self.make(way, k, True).wait_send()
                for i in range(3):
                    self.pair(way, k, i, self.view).wait_send()


class Plane:
    def __init__(self, view, src, a, b, a_dev, b_dev, sems):
        self.view, self.src, self.a, self.b = view, src, a, b
        self.a_dev, self.b_dev = a_dev, b_dev
        self.sa, self.ra, self.sb, self.rb = sems
        self.drains = []

    def go(self, src, dst, send, recv, to):
        make = lambda: remote(src, dst, send, recv, to)
        make().start()
        self.drains.append(lambda: make().wait_send())

    def wait(self, dst, recv, to):
        remote(dst, dst, recv, recv, to).wait_recv()

    def near(self, at, way):
        return (at + (1 if way == 0 else 3)) % 4

    def entry(self, j):
        at = [self.a, self.near(self.a, 1), self.near(self.a, 0)] + [(self.a + 2) % 4] * 2
        return at[j], (None if j < 3 else j - 3)

    def send_a(self):
        own = self.view(self.a, self.b)
        for way in (0, 1):
            self.go(
                self.src, own, self.sa.at[0, way], self.ra.at[0, way],
                self.a_dev(self.near(self.a, way)),
            )

    def send_b(self, j, src=None):
        at, half = self.entry(j)
        part = self.view(at, self.b, half)
        for way in (0, 1):
            self.go(
                part if src is None else src, part, self.sb.at[0, way, j], self.rb.at[0, way, j],
                self.b_dev(self.near(self.b, way)),
            )

    def pass_a(self):
        for way in (0, 1):
            at = self.near(self.a, 1 - way)
            self.wait(self.view(at, self.b), self.ra.at[0, way], self.a_dev(at))
            half = self.view(at, self.b, way)
            self.go(
                half, half, self.sa.at[1, way], self.ra.at[1, way],
                self.a_dev(self.near(self.a, way)),
            )
            self.send_b(1 + way)

    def pass_far(self):
        far = (self.a + 2) % 4
        for way in (0, 1):
            self.wait(self.view(far, self.b, way), self.ra.at[1, way], self.a_dev(far))
            self.send_b(3 + way)

    def pass_b(self, j):
        at, half = self.entry(j)
        for way in (0, 1):
            near = self.near(self.b, 1 - way)
            self.wait(self.view(at, near, half), self.rb.at[0, way, j], self.b_dev(near))
            if half is None or half == way:
                part = self.view(at, near, way)
                self.go(
                    part, part, self.sb.at[1, way, j], self.rb.at[1, way, j],
                    self.b_dev(self.near(self.b, way)),
                )

    def end_b(self, j):
        at, half = self.entry(j)
        far = (self.b + 2) % 4
        for way in (0, 1):
            if half is None or half == way:
                self.wait(self.view(at, far, way), self.rb.at[1, way, j], self.b_dev(far))


class Twin:
    def __init__(self, ring, other, send, recv, dev):
        self.ring, self.other, self.sems, self.dev = ring, other, (send, recv), dev

    def make(self, way, step, half, view):
        part = view(self.ring.block(way, step + 1), half)
        return remote(
            part, part, self.sems[0].at[way, step, half], self.sems[1].at[way, step, half], self.dev
        )

    def __call__(self, way, step, half):
        self.make(way, step, half, self.ring.view).start()

    def each(self, steps):
        return [(way, step, half) for step in steps for way, half in self.ring.items(step)]

    def wait_recv(self, steps):
        for item in self.each(steps):
            self.make(*item, self.other).wait_recv()

    def drain(self):
        for item in self.each(range(4)):
            self.make(*item, self.ring.view).wait_send()


def rows_of(start, size, unit):
    return pl.ds(pl.multiple_of(start, unit), size)


def kernel(
    spans, lens, px, rx, gain, qg, kg, inv, wq, wkv, wo,
    po, ro,
    xr, nb, wqb, wkb, wob, wkl, accq, acck, cosb, sinb, rpos, kpos, qb, kvp, kvr, atts, attb,
    osend, ry, xs, xrx,
    loc, xas, xar, xbs, xbr, gs, gr, ks, kr, qrs, qrr, krs, krr, ors, orr, ots, otr, o1,
    nbs, nbr, kvs, kvrv, vrs, vrr, vts, vtr, ats, atr, ys, yr, zs, zr,
):
    ctx, tp = lax.axis_index("ctx"), lax.axis_index("tp")
    low, z, c = ctx // 16, (ctx // 2) % 8, ctx % 2
    hi, y = tp // 4, tp % 4
    x = hi * 2 + low
    olow, oc = 1 - low, 1 - c

    def dev(low_, z_, c_, hi_, y_):
        return (low_ * 16 + z_ * 2 + c_, hi_ * 4 + y_)

    def at_x(x_):
        return dev(x_ % 2, z, c, x_ // 2, y)

    def at_y(y_):
        return dev(low, z, c, hi, y_)

    def at_g(low_, c_):
        return dev(low_, z, c_, hi, y)

    x_up, x_dn, x_far = (x + 1) % 4, (x + 3) % 4, (x + 2) % 4
    y_up, y_dn, y_far = (y + 1) % 4, (y + 3) % 4, (y + 2) % 4
    z_up = dev(low, (z + 1) % 8, c, hi, y)
    z_dn = dev(low, (z + 7) % 8, c, hi, y)
    twin = at_g(low, oc)
    group = [(low, oc), (olow, c), (olow, oc)]

    partners = [at_g(*m) for m in group] + [z_up, z_dn]
    partners += [at_y(y_up), at_y(y_dn), at_y(y_far)]
    partners += [dev(low, (z + 2) % 8, c, hi, y), dev(low, (z + 6) % 8, c, hi, y)]
    partners += [dev(low, z, c, 1 - hi, y), dev(olow, z, c, 1 - hi, y)]
    barrier = pltpu.get_barrier_semaphore()
    for partner in partners:
        pl.semaphore_signal(barrier, inc=1, device_id=partner, device_id_type=MESH)
    for kind in range(2):
        wkl[kind] = wkv[:, kind, :]
    pl.semaphore_wait(barrier, len(partners))

    drains = []

    def finish():
        for drain in drains:
            drain()

    def block_of(part, x_, y_, half=None):
        first, count = (0, 64) if half is None else (half * 32, 32)
        return xr.at[
            part, rows_of((x_ % 2) * 64 + first, count, 32),
            rows_of(((x_ // 2) * 4 + y_) * 640, 640, 128),
        ]

    prompts = Plane(
        lambda a, b, h=None: block_of(0, a, b, h), px, x, y, at_x, at_y,
        (xas.at[0], xar.at[0], xbs.at[0], xbr.at[0]),
    )
    answers = Plane(
        lambda a, b, h=None: block_of(1, b, a, h), rx, y, x, at_y, at_x,
        (xas.at[1], xar.at[1], xbs.at[1], xbr.at[1]),
    )
    planes = (prompts, answers)
    own0, own1 = block_of(0, x, y), block_of(1, x, y)

    group4 = [(low, c)] + group

    def piece(buf, z_, low_, c_):
        return buf.at[rows_of(low_ * 2560 + z_ * 320 + c_ * 160, 160, 32)]

    def wq_cols(low_, c_):
        return wq.at[:, rows_of((low_ * 2 + c_) * 256, 256, 256)]

    def wq_send(i):
        low_, c_ = group[i]
        return remote(
            wq_cols(low_, c_), piece(wqb, z, low, c), gs.at[i], gr.at[i], at_g(low_, c_)
        )

    def wk_cols(low_):
        return wkl.at[low_]

    def wk_send(i, low_):
        return remote(wk_cols(low_), piece(wkb, z, low, c), ks.at[i], kr.at[i], at_g(low_, 0))

    qring = Ring(
        lambda z_, p: piece(wqb, z_, *group4[p]), qrs, qrr, z, z_up, z_dn, 4
    )
    kring = Ring(
        lambda z_, p: piece(wkb, z_, *group4[p]), krs, krr, z, z_up, z_dn, 4
    )

    def if_keys(run):
        pl.when(c == 0)(run)

    prompts.send_a()
    prompts.send_b(0, px)

    @pl.when(c == 0)
    def _():
        kring.start(0, wk_cols(low))
        wk_send(1, olow).start()
        pltpu.make_async_copy(wk_cols(low), piece(wkb, z, low, c), loc.at[3]).start()

    @pl.when(c == 1)
    def _():
        wk_send(0, low).start()
        wk_send(2, olow).start()

    for i in range(3):
        wq_send(i).start()
    qring.start(0, wq_cols(low, c))
    answers.send_a()
    answers.send_b(0, rx)

    local0 = pltpu.make_async_copy(px, own0, loc.at[0])
    local1 = pltpu.make_async_copy(rx, own1, loc.at[1])
    local2 = pltpu.make_async_copy(wq_cols(low, c), piece(wqb, z, low, c), loc.at[2])
    local0.start()
    local1.start()
    local2.start()

    def wo_view(c_):
        return lambda z_, h: wob.at[rows_of(z_ * 320 + c_ * 160 + h * 80, 80, 16)]

    wo_own = wob.at[rows_of(z * 320 + c * 160, 160, 32)]
    local4 = pltpu.make_async_copy(wo, wo_own, loc.at[4])
    local4.start()

    oring = Ring(wo_view(c), ors, orr, z, z_up, z_dn)
    otwin = Twin(oring, wo_view(oc), ots, otr, twin)
    for h in range(2):
        oring.start(h, wo.at[pl.ds(h * 80, 80)])
    remote(wo, wo_own, o1.at[0], o1.at[1], twin).start()
    drains.append(lambda: remote(wo_own, wo_own, o1.at[0], o1.at[1], twin).wait_send())
    drains.append(oring.drain)
    drains.append(otwin.drain)

    @if_keys
    def _():
        for i in range(3):
            here = piece(wkb, z, *group[i])
            remote(here, here, ks.at[i], kr.at[i], twin).wait_recv()
            kring.start(i + 1)

    prompts.pass_a()
    prompts.pass_b(0)
    for i in range(3):
        here = piece(wqb, z, *group[i])
        remote(here, here, gs.at[i], gr.at[i], twin).wait_recv()
        qring.start(i + 1)
    prompts.pass_far()
    if_keys(lambda: kring.forward(1))
    answers.pass_a()
    qring.forward(1, parts=(0,))
    prompts.pass_b(1)
    prompts.pass_b(2)
    if_keys(lambda: kring.forward(2))
    prompts.pass_b(3)
    prompts.pass_b(4)
    answers.pass_b(0)
    answers.pass_far()
    qring.forward(1, parts=(1, 2, 3))
    if_keys(lambda: kring.forward(3))

    iota = lax.broadcasted_iota(jnp.int32, (32, 128), 0)
    for c_ in range(2):
        for low_ in range(2):
            for h in range(2):
                sid = spans[2 * (low_ * 16 + z * 2 + c_) + h]
                first = c_ * 128 + low_ * 64 + h * 32
                rpos[pl.ds(first, 32), :] = (sid * 32 + iota).astype(F32)
                rpos[pl.ds(256 + first, 32), :] = (2048 + c_ * 64 + h * 32 + iota).astype(F32)
    first_half = lax.broadcasted_iota(jnp.int32, (128, 128), 1) < 64

    @pl.loop(0, 4)
    def _(i):
        rows = rows_of(i * 128, 128, 128)
        angles = rpos[rows, :] * inv[...]
        cosb[rows, :] = jnp.cos(angles)
        sine = jnp.sin(angles)
        sinb[rows, :] = jnp.where(first_half, -sine, sine)

    for copy in (local0, local1, local2, local4):
        copy.wait()
    for j in range(5):
        prompts.end_b(j)

    drains.append(lambda: [drain() for plane in planes for drain in plane.drains])
    drains.append(qring.drain)
    drains.append(lambda: [wq_send(i).wait_send() for i in range(3)])

    def drain_keys():
        @pl.when(c == 0)
        def _():
            kring.drain()
            wk_send(1, olow).wait_send()

        @pl.when(c == 1)
        def _():
            wk_send(0, low).wait_send()
            wk_send(2, olow).wait_send()

    drains.append(drain_keys)

    def normed(c_, g):
        return nb.at[rows_of((g // 2) * 256 + c_ * 128 + (g % 2) * 64, 64, 64)]

    def norm_send(c_, g):
        return remote(normed(c_, g), normed(c_, g), nbs.at[g], nbr.at[g], twin)

    def norm(g):
        @pl.loop(0, 4)
        def _(i):
            rows = xr[g // 2, rows_of((g % 2) * 64 + i * 16, 16, 16), :].astype(F32)
            mean = jnp.mean(rows * rows, axis=-1, keepdims=True)
            first = (g // 2) * 256 + c * 128 + (g % 2) * 64 + i * 16
            nb[rows_of(first, 16, 16), :] = (
                rows * lax.rsqrt(mean + 1e-06) * gain[...]
            ).astype(BF)

        norm_send(c, g).start()

    drains.append(lambda: [norm_send(c, g).wait_send() for g in range(4)])
    norm(0)
    norm(1)
    if_keys(kring.last)
    if_keys(lambda: pltpu.make_async_copy(wk_cols(low), piece(wkb, z, low, c), loc.at[3]).wait())
    qring.forward(2, parts=(0,))
    for j in range(1, 5):
        answers.pass_b(j)
    for g in range(2):
        norm_send(oc, g).wait_recv()

    def head(values, gains, rows):
        mean = jnp.mean(values * values, axis=-1, keepdims=True)
        values = values * lax.rsqrt(mean + 1e-06) * gains[...]
        return values * cosb[rows, :] + pltpu.roll(values, 64, 1) * sinb[rows, :]

    def kv_send(i, p):
        low_, c_ = group[i]
        own = kvp.at[low, rows_of(z * 256, 256, 256)] if p == 0 else kvr.at[low]
        return remote(
            own, own, kvs.at[i, p], kvrv.at[0 if i == 0 else 1, p], at_g(low_, c_)
        )

    def keys(p):
        rows = pl.ds(p * 256, 256)
        acck[rows, :] = jnp.zeros((256, 128), F32)

        @pl.loop(0, 10)
        def _(i):
            part = rows_of(i * 512, 512, 512)
            acck[rows, :] += jnp.dot(nb[rows, part], wkb[part, :], preferred_element_type=F32)

        raw = acck[rows, :]
        mine = jnp.where(low == 0, head(raw, kg, rows), raw).astype(BF)
        if p == 0:
            kvp[low, rows_of(z * 256, 256, 256), :] = mine
        else:
            kvr[low] = mine
        for k in (1, 2, 0):
            kv_send(k, p).start()

    if_keys(lambda: keys(0))
    qring.forward(2, parts=(1, 2, 3))
    for j in range(5):
        answers.end_b(j)
    norm(2)
    norm(3)

    def drain_kv():
        @pl.when(c == 0)
        def _():
            for p in range(2):
                for i in range(3):
                    kv_send(i, p).wait_send()

    drains.append(drain_kv)

    def kv_wait(kind, i, p):
        part = kvp.at[kind, rows_of(z * 256, 256, 256)] if p == 0 else kvr.at[kind]
        remote(part, part, kvs.at[0, p], kvrv.at[i, p], twin).wait_recv()

    lane = lax.broadcasted_iota(jnp.int32, (8, 2048), 1)

    def key_positions(j, held):
        z_, c_, low_, h = j // 8, (j // 4) % 2, (j // 2) % 2, j % 2
        sid = spans[2 * (low_ * 16 + z_ * 2 + c_) + h]
        return jnp.where(lane // 32 == j, sid * 32 + lane % 32, held)

    kpos[...] = lax.fori_loop(
        0, 64, key_positions, jnp.zeros((8, 2048), jnp.int32)
    ).astype(F32)
    pl.when(c == 1)(lambda: kv_wait(low, 0, 0))
    kv_wait(olow, 1, 0)

    def kv_view(low_, kind):
        def view(z_, h):
            first, count = (0, 128) if h is None else (h * 64, 64)
            return kvp.at[kind, rows_of(z_ * 256 + low_ * 128 + first, count, 64)]

        return view

    spread = Spread(
        kv_view(low, c), [kv_view(*m) for m in group], (vrs, vrr, vts, vtr), z,
        lambda z_: dev(low, z_, c, hi, y), [at_g(*m) for m in group],
    )
    spread.start()
    drains.append(spread.drain)
    qring.forward(3)
    oring.forward(1, otwin, (0,))
    for g in (2, 3):
        norm_send(oc, g).wait_recv()
    spread.middle()
    if_keys(lambda: keys(1))
    oring.forward(1, otwin, (1,))
    qring.last()
    accq[...] = jnp.zeros_like(accq)

    @pl.loop(0, 10)
    def _(i):
        part = rows_of(i * 512, 512, 512)
        accq[...] += jnp.dot(nb[:, part], wqb[part, :], preferred_element_type=F32)

    spread.last()
    for i in range(4):
        rows = pl.ds(i * 128, 128)
        for h in range(2):
            qb[i, pl.ds(h * 128, 128), :] = head(
                accq[rows, pl.ds(h * 128, 128)], qg, rows
            ).astype(BF)
    pl.when(c == 1)(lambda: kv_wait(low, 0, 1))
    kv_wait(olow, 1, 1)
    spread.twins()

    scale = 128 ** (-0.5)

    def attend(c_, p):
        queries = qb[p * 2 + c_]
        scores = lax.dot_general(queries, kvp[0], NT, preferred_element_type=F32) * scale
        if p == 0:
            mine = rpos[rows_of(c_ * 128, 128, 128), :][:, :1]
            allowed = kpos[:1, :] <= jnp.concatenate([mine, mine], axis=0)
            scores = jnp.where(allowed, scores, -1e30)
        peak = jnp.max(scores, axis=-1, keepdims=True)
        if p == 1:
            own = lax.dot_general(queries, kvr[0], NT, preferred_element_type=F32) * scale
            q_row = lax.broadcasted_iota(jnp.int32, (256, 256), 0) % 128
            k_row = lax.broadcasted_iota(jnp.int32, (256, 256), 1)
            allowed = ((q_row // 64) == ((k_row // 64) % 2)) & (
                (k_row // 128) * 64 + k_row % 64 <= c_ * 64 + q_row % 64
            )
            own = jnp.where(allowed, own, -1e30)
            peak = jnp.maximum(peak, jnp.max(own, axis=-1, keepdims=True))
        weights = jnp.exp(scores - peak)
        total = jnp.sum(weights, axis=-1, keepdims=True)
        summed = jnp.dot(weights.astype(BF), kvp[1], preferred_element_type=F32)
        if p == 1:
            more = jnp.exp(own - peak)
            total = total + jnp.sum(more, axis=-1, keepdims=True)
            summed = summed + jnp.dot(more.astype(BF), kvr[1], preferred_element_type=F32)
        result = (summed / total).astype(BF)
        for h in range(2):
            atts[c_, pl.ds(p * 128, 128), pl.ds(h * 128, 128)] = result[h * 128 : (h + 1) * 128]

    def att_cols(low_, c_):
        return attb.at[:, rows_of((low_ * 2 + c_) * 256, 256, 256)]

    def att_send(i):
        low_, c_ = group[i]
        return remote(atts.at[c_], att_cols(low, c), ats.at[i], atr.at[i], at_g(low_, c_))

    attend(oc, 0)
    attend(oc, 1)
    att_send(2).start()
    att_send(0).start()
    oring.forward(2, otwin, (0,))
    attend(c, 0)
    oring.forward(2, otwin, (1,))
    attend(c, 1)
    att_send(1).start()
    drains.append(lambda: [att_send(i).wait_send() for i in range(3)])
    attb[:, rows_of((low * 2 + c) * 256, 256, 256)] = atts[c]
    other_own = wob.at[rows_of(z * 320 + oc * 160, 160, 32)]
    remote(other_own, other_own, o1.at[0], o1.at[1], twin).wait_recv()
    otwin.wait_recv(range(2))
    for i in range(3):
        part = att_cols(*group[i])
        remote(part, part, ats.at[i], atr.at[i], twin).wait_recv()

    early, late = (1 - z % 2) * 384, (z % 2) * 256

    def cols_of(k):
        return pl.ds(0, 640) if k < 3 else (
            rows_of(early, 256, 128) if k == 3 else rows_of(late, 384, 128)
        )

    def y_send(k, p, y_):
        place = (y_ - y + 3) % 4
        rows, cols = pl.ds(p * 128, 128), cols_of(k)
        return remote(
            osend.at[min(k, 3), rows, cols], ry.at[place, rows, cols],
            ys.at[k, p], yr.at[place, p, k // 4], at_y(y_),
        )

    def y_of(k):
        return (z // 2 + (0, 3 + 2 * (z % 2), 5 - 2 * (z % 2), 2, 2)[k]) % 4

    def project(k):
        y_ = y_of(k)
        first = y_ * 640 + (0, 0, 0, early, late)[k]
        weights = wob[rows_of(first, (640, 640, 640, 256, 384)[k], 128), :]
        for p in range(2):
            rows = pl.ds(p * 128, 128)
            osend[min(k, 3), rows, cols_of(k)] = lax.dot_general(
                attb[rows, :], weights, NT, preferred_element_type=F32
            ).astype(BF)
            pl.when(y_ != y)(lambda: y_send(k, p, y_).start())

    def drain_y():
        for k in range(5):
            for p in range(2):
                pl.when(y_of(k) != y)(lambda k=k, p=p: y_send(k, p, y_of(k)).wait_send())

    drains.append(drain_y)
    project(0)
    oring.forward(3, otwin)
    project(1)
    otwin.wait_recv((2,))
    project(2)
    project(3)
    oring.last(otwin)
    otwin.wait_recv((3,))
    project(4)

    def x_send(low_, p):
        return remote(
            xs.at[pl.ds(p * 128 + low_ * 64, 64)], xrx.at[hi, p],
            zs.at[low_, p], zr.at[hi, p], dev(low_, z, c, low, y),
        )

    mine = (y - z // 2 + 4) % 4
    slot = jnp.where(mine == 2, 3, jnp.where(mine % 2 == 0, 0, 2 - (mine // 2 + z) % 2))
    for p in range(2):
        rows = pl.ds(p * 128, 128)

        def y_wait(k, p=p):
            for i in range(3):
                part = ry.at[i, pl.ds(p * 128, 128), cols_of(k)]
                remote(part, part, ys.at[0, p], yr.at[i, p, k // 4], twin).wait_recv()

        @pl.when(mine == 2)
        def _(y_wait=y_wait):
            y_wait(3)
            y_wait(4)

        pl.when(mine != 2)(lambda: y_wait(0))
        total = osend[slot, rows, :].astype(F32)
        for i in range(3):
            total += ry[i, rows, :].astype(F32)
        xs[rows, :] = total.astype(BF)
        for low_ in range(2):
            here = jnp.logical_and(hi == low, low == low_)

            @pl.when(here)
            def _(low_=low_, p=p):
                xrx[hi, p] = xs[pl.ds(p * 128 + low_ * 64, 64), :]

            pl.when(jnp.logical_not(here))(lambda low_=low_, p=p: x_send(low_, p).start())

    offsets = c * 64 + lax.broadcasted_iota(jnp.int32, (64, 640), 0)
    for p in range(2):
        for hi_ in range(2):

            @pl.when(jnp.logical_not(jnp.logical_and(hi == low, hi == hi_)))
            def _(hi_=hi_, p=p):
                part = xrx.at[hi_, p]
                remote(part, part, zs.at[0, p], zr.at[hi_, p], twin).wait_recv()

        total = xrx[0, p].astype(F32) + xrx[1, p].astype(F32)
        if p == 0:
            po[...] = total.astype(BF)
        else:
            ro[...] = jnp.where(offsets < lens[ctx // 2], total, 0.0).astype(BF)

    finish()
    for low_ in range(2):
        here = jnp.logical_and(hi == low, low == low_)

        @pl.when(jnp.logical_not(here))
        def _(low_=low_):
            for p in range(2):
                x_send(low_, p).wait_send()


def body(prompt_x, resp_x, span_ids, lengths, in_gain, q_gain, k_gain, w_query, w_keyval, w_out):
    half = 1000000.0 ** (-(np.arange(64) * 2.0) / 128)
    inverse = np.concatenate([half, half])[None, :].astype(np.float32)
    dma = pltpu.SemaphoreType.DMA
    hbm, vmem, smem = (pl.BlockSpec(memory_space=s) for s in (pl.ANY, pltpu.VMEM, pltpu.SMEM))
    out = jax.ShapeDtypeStruct((64, 640), BF)
    return pl.pallas_call(
        kernel,
        out_shape=(out, out),
        in_specs=[smem, smem, hbm, hbm, vmem, vmem, vmem, vmem, hbm, vmem, hbm],
        out_specs=(vmem, vmem),
        scratch_shapes=[
            pltpu.VMEM((2, 128, 5120), BF),
            pltpu.VMEM((512, 5120), BF),
            pltpu.VMEM((5120, 256), BF),
            pltpu.VMEM((5120, 128), BF),
            pltpu.VMEM((2560, 1024), BF),
            pltpu.VMEM((2, 160, 128), BF),
            pltpu.VMEM((512, 256), F32),
            pltpu.VMEM((512, 128), F32),
            pltpu.VMEM((512, 128), F32),
            pltpu.VMEM((512, 128), F32),
            pltpu.VMEM((512, 128), F32),
            pltpu.VMEM((8, 2048), F32),
            pltpu.VMEM((4, 256, 128), BF),
            pltpu.VMEM((2, 2048, 128), BF),
            pltpu.VMEM((2, 256, 128), BF),
            pltpu.VMEM((2, 256, 256), BF),
            pltpu.VMEM((256, 1024), BF),
            pltpu.VMEM((4, 256, 640), BF),
            pltpu.VMEM((3, 256, 640), BF),
            pltpu.VMEM((256, 640), BF),
            pltpu.VMEM((2, 2, 64, 640), BF),
            dma((5,)),
            dma((2, 2, 2)), dma((2, 2, 2)),
            dma((2, 2, 2, 5)), dma((2, 2, 2, 5)),
            dma((3,)), dma((3,)),
            dma((3,)), dma((3,)),
            dma((2, 4, 4)), dma((2, 4, 4)),
            dma((2, 4, 4)), dma((2, 4, 4)),
            dma((2, 4, 2)), dma((2, 4, 2)),
            dma((2, 4, 2)), dma((2, 4, 2)),
            dma((2,)),
            dma((4,)), dma((4,)),
            dma((3, 2)), dma((2, 2)),
            dma((2, 4)), dma((2, 4)),
            dma((3, 2, 4)), dma((3, 2, 4)),
            dma((3,)), dma((3,)),
            dma((5, 2)), dma((3, 2, 2)),
            dma((2, 2)), dma((2, 2)),
        ],
        compiler_params=pltpu.CompilerParams(
            collective_id=0, has_side_effects=True, vmem_limit_bytes=56 * 2**20
        ),
        name="attention_block",
    )(
        span_ids, lengths, prompt_x, resp_x, in_gain[None, :], q_gain[None, :], k_gain[None, :],
        inverse, w_query, w_keyval, jnp.transpose(w_out),
    )


def solution(mesh):
    placed = (
        P("ctx", "tp"),
        P("ctx", "tp"),
        P(),
        P(),
        P(),
        P(),
        P(),
        P("ctx", "tp"),
        P("ctx", None, "tp"),
        P("tp", "ctx"),
    )
    return jax.shard_map(
        body,
        mesh=mesh,
        in_specs=placed,
        out_specs=(P("ctx", "tp"), P("ctx", "tp")),
        check_vma=False,
    )
```

```python
import functools

import jax
import jax.numpy as jnp
import numpy as np
from jax import lax
from jax.experimental import pallas as pl
from jax.experimental.pallas import tpu as pltpu
from jax.sharding import PartitionSpec as P

MESH = pl.DeviceIdType.MESH
BF = jnp.bfloat16
F32 = jnp.float32
NT = (((1,), (1,)), ((), ()))


def remote(src, dst, send, recv, dev):
    return pltpu.make_async_remote_copy(
        src_ref=src, dst_ref=dst, send_sem=send, recv_sem=recv, device_id=dev, device_id_type=MESH
    )


class Ring:
    def __init__(self, view, send, recv, z, up_dev, down_dev, parts=2):
        self.view, self.send, self.recv, self.z, self.parts = view, send, recv, z, parts
        self.devs = (up_dev, down_dev)

    def items(self, step):
        every = [(way, part) for part in range(self.parts) for way in (0, 1)]
        return every if step < 3 else [i for i in every if i[0] == i[1] * 2 // self.parts]

    def block(self, way, step):
        return lax.rem(self.z + (8 - step if way == 0 else step), 8)

    def copy(self, way, step, part, src=None):
        there = self.view(self.block(way, step), part)
        return remote(
            there if src is None else src, there,
            self.send.at[way, step, part], self.recv.at[way, step, part], self.devs[way],
        )

    def arrived(self, way, step, part):
        here = self.view(self.block(way, step + 1), part)
        remote(
            here, here, self.send.at[way, step, part], self.recv.at[way, step, part],
            self.devs[way],
        ).wait_recv()

    def start(self, part, src=None):
        for way in (0, 1):
            self.copy(way, 0, part, src).start()

    def forward(self, step, then=None, parts=None):
        for way, part in self.items(step - 1):
            if parts is not None and part not in parts:
                continue
            self.arrived(way, step - 1, part)
            if step < 4 and (way, part) in self.items(step):
                self.copy(way, step, part).start()
            if then is not None:
                then(way, step - 1, part)

    def last(self, then=None):
        self.forward(4, then)

    def drain(self):
        for step in range(4):
            for way, part in self.items(step):
                self.copy(way, step, part).wait_send()


class Plane:
    def __init__(self, view, src, a, b, a_dev, b_dev, sems):
        self.view, self.src, self.a, self.b = view, src, a, b
        self.a_dev, self.b_dev = a_dev, b_dev
        self.sa, self.ra, self.sb, self.rb = sems
        self.drains = []

    def go(self, src, dst, send, recv, to):
        make = lambda: remote(src, dst, send, recv, to)
        make().start()
        self.drains.append(lambda: make().wait_send())

    def wait(self, dst, recv, to):
        remote(dst, dst, recv, recv, to).wait_recv()

    def near(self, at, way):
        return (at + (1 if way == 0 else 3)) % 4

    def entry(self, j):
        at = [self.a, self.near(self.a, 1), self.near(self.a, 0)] + [(self.a + 2) % 4] * 2
        return at[j], (None if j < 3 else j - 3)

    def send_a(self):
        own = self.view(self.a, self.b)
        for way in (0, 1):
            self.go(
                self.src, own, self.sa.at[0, way], self.ra.at[0, way],
                self.a_dev(self.near(self.a, way)),
            )

    def send_b(self, j, src=None):
        at, half = self.entry(j)
        part = self.view(at, self.b, half)
        for way in (0, 1):
            self.go(
                part if src is None else src, part, self.sb.at[0, way, j], self.rb.at[0, way, j],
                self.b_dev(self.near(self.b, way)),
            )

    def pass_a(self):
        for way in (0, 1):
            at = self.near(self.a, 1 - way)
            self.wait(self.view(at, self.b), self.ra.at[0, way], self.a_dev(at))
            half = self.view(at, self.b, way)
            self.go(
                half, half, self.sa.at[1, way], self.ra.at[1, way],
                self.a_dev(self.near(self.a, way)),
            )
            self.send_b(1 + way)

    def pass_far(self):
        far = (self.a + 2) % 4
        for way in (0, 1):
            self.wait(self.view(far, self.b, way), self.ra.at[1, way], self.a_dev(far))
            self.send_b(3 + way)

    def pass_b(self, j):
        at, half = self.entry(j)
        for way in (0, 1):
            near = self.near(self.b, 1 - way)
            self.wait(self.view(at, near, half), self.rb.at[0, way, j], self.b_dev(near))
            if half is None or half == way:
                part = self.view(at, near, way)
                self.go(
                    part, part, self.sb.at[1, way, j], self.rb.at[1, way, j],
                    self.b_dev(self.near(self.b, way)),
                )

    def end_b(self, j):
        at, half = self.entry(j)
        far = (self.b + 2) % 4
        for way in (0, 1):
            if half is None or half == way:
                self.wait(self.view(at, far, way), self.rb.at[1, way, j], self.b_dev(far))


class Spread:
    def __init__(self, view, others, sems, z, to_z, devs):
        self.view, self.others, self.z, self.to_z, self.devs = view, others, z, to_z, devs
        self.send, self.recv, self.tsend, self.trecv = sems

    def make(self, way, k, sender):
        sign = 1 if way == 0 else -1
        hops, owner = ((1, 0), (2, 0), (1, 2), (2, 2))[k]
        start = self.z if sender else self.z - sign * hops
        block = (start - sign * owner + 16) % 8
        part = self.view(block, way if k == 3 else None)
        return remote(
            part, part, self.send.at[way, k], self.recv.at[way, k],
            self.to_z((self.z + sign * hops + 8) % 8),
        )

    def pair(self, way, k, i, view):
        sign = 1 if way == 0 else -1
        block = (self.z - sign * (k + 1) + 16) % 8
        part = view(block, way if k == 3 else None)
        return remote(
            part, part, self.tsend.at[i, way, k], self.trecv.at[i, way, k], self.devs[i]
        )

    def start(self):
        for k in (1, 0):
            for way in (0, 1):
                self.make(way, k, True).start()

    def arrive(self, way, k):
        self.make(way, k, False).wait_recv()
        for i in (1, 2, 0):
            self.pair(way, k, i, self.view).start()

    def middle(self):
        for way in (0, 1):
            self.arrive(way, 1)
            self.make(way, 3, True).start()
            self.make(way, 2, True).start()
        for way in (0, 1):
            self.arrive(way, 0)

    def last(self):
        for k in (3, 2):
            for way in (0, 1):
                self.arrive(way, k)

    def twins(self):
        for k in range(4):
            for way in (0, 1):
                for i in range(3):
                    self.pair(way, k, i, self.others[i]).wait_recv()

    def drain(self):
        for k in range(4):
            for way in (0, 1):
                self.make(way, k, True).wait_send()
                for i in range(3):
                    self.pair(way, k, i, self.view).wait_send()


class Plane:
    def __init__(self, view, src, a, b, a_dev, b_dev, sems):
        self.view, self.src, self.a, self.b = view, src, a, b
        self.a_dev, self.b_dev = a_dev, b_dev
        self.sa, self.ra, self.sb, self.rb = sems
        self.drains = []

    def go(self, src, dst, send, recv, to):
        make = lambda: remote(src, dst, send, recv, to)
        make().start()
        self.drains.append(lambda: make().wait_send())

    def wait(self, dst, recv, to):
        remote(dst, dst, recv, recv, to).wait_recv()

    def near(self, at, way):
        return (at + (1 if way == 0 else 3)) % 4

    def entry(self, j):
        at = [self.a, self.near(self.a, 1), self.near(self.a, 0)] + [(self.a + 2) % 4] * 2
        return at[j], (None if j < 3 else j - 3)

    def send_a(self):
        own = self.view(self.a, self.b)
        for way in (0, 1):
            self.go(
                self.src, own, self.sa.at[0, way], self.ra.at[0, way],
                self.a_dev(self.near(self.a, way)),
            )

    def send_b(self, j, src=None):
        at, half = self.entry(j)
        part = self.view(at, self.b, half)
        for way in (0, 1):
            self.go(
                part if src is None else src, part, self.sb.at[0, way, j], self.rb.at[0, way, j],
                self.b_dev(self.near(self.b, way)),
            )

    def pass_a(self):
        for way in (0, 1):
            at = self.near(self.a, 1 - way)
            self.wait(self.view(at, self.b), self.ra.at[0, way], self.a_dev(at))
            half = self.view(at, self.b, way)
            self.go(
                half, half, self.sa.at[1, way], self.ra.at[1, way],
                self.a_dev(self.near(self.a, way)),
            )
            self.send_b(1 + way)

    def pass_far(self):
        far = (self.a + 2) % 4
        for way in (0, 1):
            self.wait(self.view(far, self.b, way), self.ra.at[1, way], self.a_dev(far))
            self.send_b(3 + way)

    def pass_b(self, j):
        at, half = self.entry(j)
        for way in (0, 1):
            near = self.near(self.b, 1 - way)
            self.wait(self.view(at, near, half), self.rb.at[0, way, j], self.b_dev(near))
            if half is None or half == way:
                part = self.view(at, near, way)
                self.go(
                    part, part, self.sb.at[1, way, j], self.rb.at[1, way, j],
                    self.b_dev(self.near(self.b, way)),
                )

    def end_b(self, j):
        at, half = self.entry(j)
        far = (self.b + 2) % 4
        for way in (0, 1):
            if half is None or half == way:
                self.wait(self.view(at, far, way), self.rb.at[1, way, j], self.b_dev(far))


class Twin:
    def __init__(self, ring, other, send, recv, dev):
        self.ring, self.other, self.sems, self.dev = ring, other, (send, recv), dev

    def make(self, way, step, half, view):
        part = view(self.ring.block(way, step + 1), half)
        return remote(
            part, part, self.sems[0].at[way, step, half], self.sems[1].at[way, step, half], self.dev
        )

    def __call__(self, way, step, half):
        self.make(way, step, half, self.ring.view).start()

    def each(self, steps):
        return [(way, step, half) for step in steps for way, half in self.ring.items(step)]

    def wait_recv(self, steps):
        for item in self.each(steps):
            self.make(*item, self.other).wait_recv()

    def drain(self):
        for item in self.each(range(4)):
            self.make(*item, self.ring.view).wait_send()


def rows_of(start, size, unit):
    return pl.ds(pl.multiple_of(start, unit), size)


def kernel(
    spans, lens, px, rx, gain, qg, kg, inv, wq, wkv, wo,
    both,
    xr, nb, wqb, wkb, wob, wkl, accq, acck, cosb, sinb, rpos, kpos, qb, kvp, kvr, atts, attb,
    osend, ry, xs, xrx,
    loc, xas, xar, xbs, xbr, gs, gr, ks, kr, qrs, qrr, krs, krr, ors, orr, ots, otr, o1,
    nbs, nbr, kvs, kvrv, vrs, vrr, vts, vtr, ats, atr, ys, yr, zs, zr,
):
    ctx, tp = lax.axis_index("ctx"), lax.axis_index("tp")
    low, z, c = ctx // 16, (ctx // 2) % 8, ctx % 2
    hi, y = tp // 4, tp % 4
    x = hi * 2 + low
    olow, oc = 1 - low, 1 - c

    def dev(low_, z_, c_, hi_, y_):
        return (low_ * 16 + z_ * 2 + c_, hi_ * 4 + y_)

    def at_x(x_):
        return dev(x_ % 2, z, c, x_ // 2, y)

    def at_y(y_):
        return dev(low, z, c, hi, y_)

    def at_g(low_, c_):
        return dev(low_, z, c_, hi, y)

    x_up, x_dn, x_far = (x + 1) % 4, (x + 3) % 4, (x + 2) % 4
    y_up, y_dn, y_far = (y + 1) % 4, (y + 3) % 4, (y + 2) % 4
    z_up = dev(low, (z + 1) % 8, c, hi, y)
    z_dn = dev(low, (z + 7) % 8, c, hi, y)
    twin = at_g(low, oc)
    group = [(low, oc), (olow, c), (olow, oc)]

    partners = [at_g(*m) for m in group] + [z_up, z_dn]
    partners += [at_y(y_up), at_y(y_dn), at_y(y_far)]
    partners += [dev(low, (z + 2) % 8, c, hi, y), dev(low, (z + 6) % 8, c, hi, y)]
    partners += [dev(low, z, c, 1 - hi, y), dev(olow, z, c, 1 - hi, y)]
    barrier = pltpu.get_barrier_semaphore()
    for partner in partners:
        pl.semaphore_signal(barrier, inc=1, device_id=partner, device_id_type=MESH)
    for kind in range(2):
        wkl[kind] = wkv[:, kind, :]
    pl.semaphore_wait(barrier, len(partners))

    drains = []

    def finish():
        for drain in drains:
            drain()

    def block_of(part, x_, y_, half=None):
        first, count = (0, 64) if half is None else (half * 32, 32)
        return xr.at[
            part, rows_of((x_ % 2) * 64 + first, count, 32),
            rows_of(((x_ // 2) * 4 + y_) * 640, 640, 128),
        ]

    prompts = Plane(
        lambda a, b, h=None: block_of(0, a, b, h), px, x, y, at_x, at_y,
        (xas.at[0], xar.at[0], xbs.at[0], xbr.at[0]),
    )
    answers = Plane(
        lambda a, b, h=None: block_of(1, b, a, h), rx, y, x, at_y, at_x,
        (xas.at[1], xar.at[1], xbs.at[1], xbr.at[1]),
    )
    planes = (prompts, answers)
    own0, own1 = block_of(0, x, y), block_of(1, x, y)

    group4 = [(low, c)] + group

    def piece(buf, z_, low_, c_):
        return buf.at[rows_of(low_ * 2560 + z_ * 320 + c_ * 160, 160, 32)]

    def wq_cols(low_, c_):
        return wq.at[:, rows_of((low_ * 2 + c_) * 256, 256, 256)]

    def wq_send(i):
        low_, c_ = group[i]
        return remote(
            wq_cols(low_, c_), piece(wqb, z, low, c), gs.at[i], gr.at[i], at_g(low_, c_)
        )

    def wk_cols(low_):
        return wkl.at[low_]

    def wk_send(i, low_):
        return remote(wk_cols(low_), piece(wkb, z, low, c), ks.at[i], kr.at[i], at_g(low_, 0))

    qring = Ring(
        lambda z_, p: piece(wqb, z_, *group4[p]), qrs, qrr, z, z_up, z_dn, 4
    )
    kring = Ring(
        lambda z_, p: piece(wkb, z_, *group4[p]), krs, krr, z, z_up, z_dn, 4
    )

    def if_keys(run):
        pl.when(c == 0)(run)

    prompts.send_a()
    prompts.send_b(0, px)

    @pl.when(c == 0)
    def _():
        kring.start(0, wk_cols(low))
        wk_send(1, olow).start()
        pltpu.make_async_copy(wk_cols(low), piece(wkb, z, low, c), loc.at[3]).start()

    @pl.when(c == 1)
    def _():
        wk_send(0, low).start()
        wk_send(2, olow).start()

    for i in range(3):
        wq_send(i).start()
    qring.start(0, wq_cols(low, c))
    answers.send_a()
    answers.send_b(0, rx)

    local0 = pltpu.make_async_copy(px, own0, loc.at[0])
    local1 = pltpu.make_async_copy(rx, own1, loc.at[1])
    local2 = pltpu.make_async_copy(wq_cols(low, c), piece(wqb, z, low, c), loc.at[2])
    local0.start()
    local1.start()
    local2.start()

    def wo_view(c_):
        return lambda z_, h: wob.at[rows_of(z_ * 320 + c_ * 160 + h * 80, 80, 16)]

    wo_own = wob.at[rows_of(z * 320 + c * 160, 160, 32)]
    local4 = pltpu.make_async_copy(wo, wo_own, loc.at[4])
    local4.start()

    oring = Ring(wo_view(c), ors, orr, z, z_up, z_dn)
    otwin = Twin(oring, wo_view(oc), ots, otr, twin)
    for h in range(2):
        oring.start(h, wo.at[pl.ds(h * 80, 80)])
    remote(wo, wo_own, o1.at[0], o1.at[1], twin).start()
    drains.append(lambda: remote(wo_own, wo_own, o1.at[0], o1.at[1], twin).wait_send())
    drains.append(oring.drain)
    drains.append(otwin.drain)

    @if_keys
    def _():
        for i in range(3):
            here = piece(wkb, z, *group[i])
            remote(here, here, ks.at[i], kr.at[i], twin).wait_recv()
            kring.start(i + 1)

    prompts.pass_a()
    prompts.pass_b(0)
    for i in range(3):
        here = piece(wqb, z, *group[i])
        remote(here, here, gs.at[i], gr.at[i], twin).wait_recv()
        qring.start(i + 1)
    prompts.pass_far()
    if_keys(lambda: kring.forward(1))
    answers.pass_a()
    qring.forward(1, parts=(0,))
    prompts.pass_b(1)
    prompts.pass_b(2)
    if_keys(lambda: kring.forward(2))
    prompts.pass_b(3)
    prompts.pass_b(4)
    answers.pass_b(0)
    answers.pass_far()
    qring.forward(1, parts=(1, 2, 3))
    if_keys(lambda: kring.forward(3))

    iota = lax.broadcasted_iota(jnp.int32, (32, 128), 0)
    for c_ in range(2):
        for low_ in range(2):
            for h in range(2):
                sid = spans[2 * (low_ * 16 + z * 2 + c_) + h]
                first = c_ * 128 + low_ * 64 + h * 32
                rpos[pl.ds(first, 32), :] = (sid * 32 + iota).astype(F32)
                rpos[pl.ds(256 + first, 32), :] = (2048 + c_ * 64 + h * 32 + iota).astype(F32)
    first_half = lax.broadcasted_iota(jnp.int32, (128, 128), 1) < 64

    @pl.loop(0, 4)
    def _(i):
        rows = rows_of(i * 128, 128, 128)
        angles = rpos[rows, :] * inv[...]
        cosb[rows, :] = jnp.cos(angles)
        sine = jnp.sin(angles)
        sinb[rows, :] = jnp.where(first_half, -sine, sine)

    for copy in (local0, local1, local2, local4):
        copy.wait()
    for j in range(5):
        prompts.end_b(j)

    drains.append(lambda: [drain() for plane in planes for drain in plane.drains])
    drains.append(qring.drain)
    drains.append(lambda: [wq_send(i).wait_send() for i in range(3)])

    def drain_keys():
        @pl.when(c == 0)
        def _():
            kring.drain()
            wk_send(1, olow).wait_send()

        @pl.when(c == 1)
        def _():
            wk_send(0, low).wait_send()
            wk_send(2, olow).wait_send()

    drains.append(drain_keys)

    def normed(c_, g):
        return nb.at[rows_of((g // 2) * 256 + c_ * 128 + (g % 2) * 64, 64, 64)]

    def norm_send(c_, g):
        return remote(normed(c_, g), normed(c_, g), nbs.at[g], nbr.at[g], twin)

    def norm(g):
        @pl.loop(0, 4)
        def _(i):
            rows = xr[g // 2, rows_of((g % 2) * 64 + i * 16, 16, 16), :].astype(F32)
            mean = jnp.mean(rows * rows, axis=-1, keepdims=True)
            first = (g // 2) * 256 + c * 128 + (g % 2) * 64 + i * 16
            nb[rows_of(first, 16, 16), :] = (
                rows * lax.rsqrt(mean + 1e-06) * gain[...]
            ).astype(BF)

        norm_send(c, g).start()

    drains.append(lambda: [norm_send(c, g).wait_send() for g in range(4)])
    norm(0)
    norm(1)
    if_keys(kring.last)
    if_keys(lambda: pltpu.make_async_copy(wk_cols(low), piece(wkb, z, low, c), loc.at[3]).wait())
    qring.forward(2, parts=(0,))
    for j in range(1, 5):
        answers.pass_b(j)
    for g in range(2):
        norm_send(oc, g).wait_recv()

    def head(values, gains, rows):
        mean = jnp.mean(values * values, axis=-1, keepdims=True)
        values = values * lax.rsqrt(mean + 1e-06) * gains[...]
        return values * cosb[rows, :] + pltpu.roll(values, 64, 1) * sinb[rows, :]

    def kv_send(i, p):
        low_, c_ = group[i]
        own = kvp.at[low, rows_of(z * 256, 256, 256)] if p == 0 else kvr.at[low]
        return remote(
            own, own, kvs.at[i, p], kvrv.at[0 if i == 0 else 1, p], at_g(low_, c_)
        )

    def keys(p):
        rows = pl.ds(p * 256, 256)
        acck[rows, :] = jnp.zeros((256, 128), F32)

        @pl.loop(0, 10)
        def _(i):
            part = rows_of(i * 512, 512, 512)
            acck[rows, :] += jnp.dot(nb[rows, part], wkb[part, :], preferred_element_type=F32)

        raw = acck[rows, :]
        mine = jnp.where(low == 0, head(raw, kg, rows), raw).astype(BF)
        if p == 0:
            kvp[low, rows_of(z * 256, 256, 256), :] = mine
        else:
            kvr[low] = mine
        for k in (1, 2, 0):
            kv_send(k, p).start()

    if_keys(lambda: keys(0))
    qring.forward(2, parts=(1, 2, 3))
    for j in range(5):
        answers.end_b(j)
    norm(2)
    norm(3)

    def drain_kv():
        @pl.when(c == 0)
        def _():
            for p in range(2):
                for i in range(3):
                    kv_send(i, p).wait_send()

    drains.append(drain_kv)

    def kv_wait(kind, i, p):
        part = kvp.at[kind, rows_of(z * 256, 256, 256)] if p == 0 else kvr.at[kind]
        remote(part, part, kvs.at[0, p], kvrv.at[i, p], twin).wait_recv()

    lane = lax.broadcasted_iota(jnp.int32, (8, 2048), 1)

    def key_positions(j, held):
        z_, c_, low_, h = j // 8, (j // 4) % 2, (j // 2) % 2, j % 2
        sid = spans[2 * (low_ * 16 + z_ * 2 + c_) + h]
        return jnp.where(lane // 32 == j, sid * 32 + lane % 32, held)

    kpos[...] = lax.fori_loop(
        0, 64, key_positions, jnp.zeros((8, 2048), jnp.int32)
    ).astype(F32)
    pl.when(c == 1)(lambda: kv_wait(low, 0, 0))
    kv_wait(olow, 1, 0)

    def kv_view(low_, kind):
        def view(z_, h):
            first, count = (0, 128) if h is None else (h * 64, 64)
            return kvp.at[kind, rows_of(z_ * 256 + low_ * 128 + first, count, 64)]

        return view

    spread = Spread(
        kv_view(low, c), [kv_view(*m) for m in group], (vrs, vrr, vts, vtr), z,
        lambda z_: dev(low, z_, c, hi, y), [at_g(*m) for m in group],
    )
    spread.start()
    drains.append(spread.drain)
    qring.forward(3)
    oring.forward(1, otwin, (0,))
    for g in (2, 3):
        norm_send(oc, g).wait_recv()
    spread.middle()
    oring.forward(1, otwin, (1,))
    if_keys(lambda: keys(1))
    qring.last()
    accq[...] = jnp.zeros_like(accq)

    @pl.loop(0, 10)
    def _(i):
        part = rows_of(i * 512, 512, 512)
        accq[...] += jnp.dot(nb[:, part], wqb[part, :], preferred_element_type=F32)

    spread.last()
    oring.forward(2, otwin, (0,))
    for i in range(4):
        rows = pl.ds(i * 128, 128)
        for h in range(2):
            qb[i, pl.ds(h * 128, 128), :] = head(
                accq[rows, pl.ds(h * 128, 128)], qg, rows
            ).astype(BF)
    pl.when(c == 1)(lambda: kv_wait(low, 0, 1))
    kv_wait(olow, 1, 1)
    spread.twins()

    scale = 128 ** (-0.5)

    def attend(c_, p):
        queries = qb[p * 2 + c_]
        scores = lax.dot_general(queries, kvp[0], NT, preferred_element_type=F32) * scale
        if p == 0:
            mine = rpos[rows_of(c_ * 128, 128, 128), :][:, :1]
            allowed = kpos[:1, :] <= jnp.concatenate([mine, mine], axis=0)
            scores = jnp.where(allowed, scores, -1e30)
        peak = jnp.max(scores, axis=-1, keepdims=True)
        if p == 1:
            own = lax.dot_general(queries, kvr[0], NT, preferred_element_type=F32) * scale
            q_row = lax.broadcasted_iota(jnp.int32, (256, 256), 0) % 128
            k_row = lax.broadcasted_iota(jnp.int32, (256, 256), 1)
            allowed = ((q_row // 64) == ((k_row // 64) % 2)) & (
                (k_row // 128) * 64 + k_row % 64 <= c_ * 64 + q_row % 64
            )
            own = jnp.where(allowed, own, -1e30)
            peak = jnp.maximum(peak, jnp.max(own, axis=-1, keepdims=True))
        weights = jnp.exp(scores - peak)
        total = jnp.sum(weights, axis=-1, keepdims=True)
        summed = jnp.dot(weights.astype(BF), kvp[1], preferred_element_type=F32)
        if p == 1:
            more = jnp.exp(own - peak)
            total = total + jnp.sum(more, axis=-1, keepdims=True)
            summed = summed + jnp.dot(more.astype(BF), kvr[1], preferred_element_type=F32)
        result = (summed / total).astype(BF)
        for h in range(2):
            atts[c_, pl.ds(p * 128, 128), pl.ds(h * 128, 128)] = result[h * 128 : (h + 1) * 128]

    def att_cols(low_, c_):
        return attb.at[:, rows_of((low_ * 2 + c_) * 256, 256, 256)]

    def att_send(i):
        low_, c_ = group[i]
        return remote(atts.at[c_], att_cols(low, c), ats.at[i], atr.at[i], at_g(low_, c_))

    oring.forward(2, otwin, (1,))
    attend(oc, 0)
    attend(oc, 1)
    att_send(2).start()
    att_send(0).start()
    attend(c, 0)
    attend(c, 1)
    att_send(1).start()
    oring.forward(3, otwin)
    drains.append(lambda: [att_send(i).wait_send() for i in range(3)])
    attb[:, rows_of((low * 2 + c) * 256, 256, 256)] = atts[c]
    other_own = wob.at[rows_of(z * 320 + oc * 160, 160, 32)]
    remote(other_own, other_own, o1.at[0], o1.at[1], twin).wait_recv()
    otwin.wait_recv(range(2))
    for i in range(3):
        part = att_cols(*group[i])
        remote(part, part, ats.at[i], atr.at[i], twin).wait_recv()

    early, late = (1 - z % 2) * 384, (z % 2) * 256

    def cols_of(k):
        return pl.ds(0, 640) if k < 3 else (
            rows_of(early, 256, 128) if k == 3 else rows_of(late, 384, 128)
        )

    def y_send(k, p, y_):
        place = (y_ - y + 3) % 4
        rows, cols = pl.ds(p * 128, 128), cols_of(k)
        return remote(
            osend.at[min(k, 3), rows, cols], ry.at[place, rows, cols],
            ys.at[k, p], yr.at[place, p, k // 4], at_y(y_),
        )

    def y_of(k):
        return (z // 2 + (0, 3 + 2 * (z % 2), 5 - 2 * (z % 2), 2, 2)[k]) % 4

    def project(k):
        y_ = y_of(k)
        first = y_ * 640 + (0, 0, 0, early, late)[k]
        weights = wob[rows_of(first, (640, 640, 640, 256, 384)[k], 128), :]
        osend[min(k, 3), :, cols_of(k)] = lax.dot_general(
            attb[...], weights, NT, preferred_element_type=F32
        ).astype(BF)
        for p in range(2):
            pl.when(y_ != y)(lambda p=p: y_send(k, p, y_).start())

    def drain_y():
        for k in range(5):
            for p in range(2):
                pl.when(y_of(k) != y)(lambda k=k, p=p: y_send(k, p, y_of(k)).wait_send())

    drains.append(drain_y)
    project(0)
    project(1)
    otwin.wait_recv((2,))
    project(2)
    project(3)
    oring.last(otwin)
    otwin.wait_recv((3,))
    project(4)

    def x_send(low_, p):
        return remote(
            xs.at[pl.ds(p * 128 + low_ * 64, 64)], xrx.at[hi, p],
            zs.at[low_, p], zr.at[hi, p], dev(low_, z, c, low, y),
        )

    mine = (y - z // 2 + 4) % 4
    slot = jnp.where(mine == 2, 3, jnp.where(mine % 2 == 0, 0, 2 - (mine // 2 + z) % 2))
    for p in range(2):
        rows = pl.ds(p * 128, 128)

        def y_wait(k, p=p):
            for i in range(3):
                part = ry.at[i, pl.ds(p * 128, 128), cols_of(k)]
                remote(part, part, ys.at[0, p], yr.at[i, p, k // 4], twin).wait_recv()

        @pl.when(mine == 2)
        def _(y_wait=y_wait):
            y_wait(3)
            y_wait(4)

        pl.when(mine != 2)(lambda: y_wait(0))
        total = osend[slot, rows, :].astype(F32)
        for i in range(3):
            total += ry[i, rows, :].astype(F32)
        xs[rows, :] = total.astype(BF)
        for low_ in range(2):
            here = jnp.logical_and(hi == low, low == low_)

            @pl.when(here)
            def _(low_=low_, p=p):
                xrx[hi, p] = xs[pl.ds(p * 128 + low_ * 64, 64), :]

            pl.when(jnp.logical_not(here))(lambda low_=low_, p=p: x_send(low_, p).start())

    offsets = c * 64 + lax.broadcasted_iota(jnp.int32, (64, 640), 0)
    for p in range(2):
        for hi_ in range(2):

            @pl.when(jnp.logical_not(jnp.logical_and(hi == low, hi == hi_)))
            def _(hi_=hi_, p=p):
                part = xrx.at[hi_, p]
                remote(part, part, zs.at[0, p], zr.at[hi_, p], twin).wait_recv()

        total = xrx[0, p].astype(F32) + xrx[1, p].astype(F32)
        if p == 0:
            both[pl.ds(0, 64), :] = total.astype(BF)
        else:
            both[pl.ds(64, 64), :] = jnp.where(offsets < lens[ctx // 2], total, 0.0).astype(BF)

    finish()
    for low_ in range(2):
        here = jnp.logical_and(hi == low, low == low_)

        @pl.when(jnp.logical_not(here))
        def _(low_=low_):
            for p in range(2):
                x_send(low_, p).wait_send()


def body(prompt_x, resp_x, span_ids, lengths, in_gain, q_gain, k_gain, w_query, w_keyval, w_out):
    half = 1000000.0 ** (-(np.arange(64) * 2.0) / 128)
    inverse = np.concatenate([half, half])[None, :].astype(np.float32)
    dma = pltpu.SemaphoreType.DMA
    hbm, vmem, smem = (pl.BlockSpec(memory_space=s) for s in (pl.ANY, pltpu.VMEM, pltpu.SMEM))
    out = jax.ShapeDtypeStruct((128, 640), BF)
    both = pl.pallas_call(
        kernel,
        out_shape=out,
        in_specs=[smem, smem, hbm, hbm, vmem, vmem, vmem, vmem, hbm, vmem, hbm],
        out_specs=vmem,
        scratch_shapes=[
            pltpu.VMEM((2, 128, 5120), BF),
            pltpu.VMEM((512, 5120), BF),
            pltpu.VMEM((5120, 256), BF),
            pltpu.VMEM((5120, 128), BF),
            pltpu.VMEM((2560, 1024), BF),
            pltpu.VMEM((2, 160, 128), BF),
            pltpu.VMEM((512, 256), F32),
            pltpu.VMEM((512, 128), F32),
            pltpu.VMEM((512, 128), F32),
            pltpu.VMEM((512, 128), F32),
            pltpu.VMEM((512, 128), F32),
            pltpu.VMEM((8, 2048), F32),
            pltpu.VMEM((4, 256, 128), BF),
            pltpu.VMEM((2, 2048, 128), BF),
            pltpu.VMEM((2, 256, 128), BF),
            pltpu.VMEM((2, 256, 256), BF),
            pltpu.VMEM((256, 1024), BF),
            pltpu.VMEM((4, 256, 640), BF),
            pltpu.VMEM((3, 256, 640), BF),
            pltpu.VMEM((256, 640), BF),
            pltpu.VMEM((2, 2, 64, 640), BF),
            dma((5,)),
            dma((2, 2, 2)), dma((2, 2, 2)),
            dma((2, 2, 2, 5)), dma((2, 2, 2, 5)),
            dma((3,)), dma((3,)),
            dma((3,)), dma((3,)),
            dma((2, 4, 4)), dma((2, 4, 4)),
            dma((2, 4, 4)), dma((2, 4, 4)),
            dma((2, 4, 2)), dma((2, 4, 2)),
            dma((2, 4, 2)), dma((2, 4, 2)),
            dma((2,)),
            dma((4,)), dma((4,)),
            dma((3, 2)), dma((2, 2)),
            dma((2, 4)), dma((2, 4)),
            dma((3, 2, 4)), dma((3, 2, 4)),
            dma((3,)), dma((3,)),
            dma((5, 2)), dma((3, 2, 2)),
            dma((2, 2)), dma((2, 2)),
        ],
        compiler_params=pltpu.CompilerParams(
            collective_id=0, has_side_effects=True, vmem_limit_bytes=56 * 2**20
        ),
        name="attention_block",
    )(
        span_ids, lengths, prompt_x, resp_x, in_gain[None, :], q_gain[None, :], k_gain[None, :],
        inverse, w_query, w_keyval, jnp.transpose(w_out),
    )
    return both[:64], both[64:]


def solution(mesh):
    placed = (
        P("ctx", "tp"),
        P("ctx", "tp"),
        P(),
        P(),
        P(),
        P(),
        P(),
        P("ctx", "tp"),
        P("ctx", None, "tp"),
        P("tp", "ctx"),
    )
    return jax.shard_map(
        body,
        mesh=mesh,
        in_specs=placed,
        out_specs=(P("ctx", "tp"), P("ctx", "tp")),
        check_vma=False,
    )
```

```python
import functools

import jax
import jax.numpy as jnp
import numpy as np
from jax import lax
from jax.experimental import pallas as pl
from jax.experimental.pallas import tpu as pltpu
from jax.sharding import PartitionSpec as P

MESH = pl.DeviceIdType.MESH
BF = jnp.bfloat16
F32 = jnp.float32
NT = (((1,), (1,)), ((), ()))


def remote(src, dst, send, recv, dev):
    return pltpu.make_async_remote_copy(
        src_ref=src, dst_ref=dst, send_sem=send, recv_sem=recv, device_id=dev, device_id_type=MESH
    )


class Ring:
    def __init__(self, view, send, recv, z, up_dev, down_dev, parts=2):
        self.view, self.send, self.recv, self.z, self.parts = view, send, recv, z, parts
        self.devs = (up_dev, down_dev)

    def items(self, step):
        every = [(way, part) for part in range(self.parts) for way in (0, 1)]
        return every if step < 3 else [i for i in every if i[0] == i[1] * 2 // self.parts]

    def block(self, way, step):
        return lax.rem(self.z + (8 - step if way == 0 else step), 8)

    def copy(self, way, step, part, src=None):
        there = self.view(self.block(way, step), part)
        return remote(
            there if src is None else src, there,
            self.send.at[way, step, part], self.recv.at[way, step, part], self.devs[way],
        )

    def arrived(self, way, step, part):
        here = self.view(self.block(way, step + 1), part)
        remote(
            here, here, self.send.at[way, step, part], self.recv.at[way, step, part],
            self.devs[way],
        ).wait_recv()

    def start(self, part, src=None):
        for way in (0, 1):
            self.copy(way, 0, part, src).start()

    def forward(self, step, then=None, parts=None):
        for way, part in self.items(step - 1):
            if parts is not None and part not in parts:
                continue
            self.arrived(way, step - 1, part)
            if step < 4 and (way, part) in self.items(step):
                self.copy(way, step, part).start()
            if then is not None:
                then(way, step - 1, part)

    def last(self, then=None):
        self.forward(4, then)

    def drain(self):
        for step in range(4):
            for way, part in self.items(step):
                self.copy(way, step, part).wait_send()


class Plane:
    def __init__(self, view, src, a, b, a_dev, b_dev, sems):
        self.view, self.src, self.a, self.b = view, src, a, b
        self.a_dev, self.b_dev = a_dev, b_dev
        self.sa, self.ra, self.sb, self.rb = sems
        self.drains = []

    def go(self, src, dst, send, recv, to):
        make = lambda: remote(src, dst, send, recv, to)
        make().start()
        self.drains.append(lambda: make().wait_send())

    def wait(self, dst, recv, to):
        remote(dst, dst, recv, recv, to).wait_recv()

    def near(self, at, way):
        return (at + (1 if way == 0 else 3)) % 4

    def entry(self, j):
        at = [self.a, self.near(self.a, 1), self.near(self.a, 0)] + [(self.a + 2) % 4] * 2
        return at[j], (None if j < 3 else j - 3)

    def send_a(self):
        own = self.view(self.a, self.b)
        for way in (0, 1):
            self.go(
                self.src, own, self.sa.at[0, way], self.ra.at[0, way],
                self.a_dev(self.near(self.a, way)),
            )

    def send_b(self, j, src=None):
        at, half = self.entry(j)
        part = self.view(at, self.b, half)
        for way in (0, 1):
            self.go(
                part if src is None else src, part, self.sb.at[0, way, j], self.rb.at[0, way, j],
                self.b_dev(self.near(self.b, way)),
            )

    def pass_a(self):
        for way in (0, 1):
            at = self.near(self.a, 1 - way)
            self.wait(self.view(at, self.b), self.ra.at[0, way], self.a_dev(at))
            half = self.view(at, self.b, way)
            self.go(
                half, half, self.sa.at[1, way], self.ra.at[1, way],
                self.a_dev(self.near(self.a, way)),
            )
            self.send_b(1 + way)

    def pass_far(self):
        far = (self.a + 2) % 4
        for way in (0, 1):
            self.wait(self.view(far, self.b, way), self.ra.at[1, way], self.a_dev(far))
            self.send_b(3 + way)

    def pass_b(self, j):
        at, half = self.entry(j)
        for way in (0, 1):
            near = self.near(self.b, 1 - way)
            self.wait(self.view(at, near, half), self.rb.at[0, way, j], self.b_dev(near))
            if half is None or half == way:
                part = self.view(at, near, way)
                self.go(
                    part, part, self.sb.at[1, way, j], self.rb.at[1, way, j],
                    self.b_dev(self.near(self.b, way)),
                )

    def end_b(self, j):
        at, half = self.entry(j)
        far = (self.b + 2) % 4
        for way in (0, 1):
            if half is None or half == way:
                self.wait(self.view(at, far, way), self.rb.at[1, way, j], self.b_dev(far))


class Spread:
    def __init__(self, view, others, sems, z, to_z, devs):
        self.view, self.others, self.z, self.to_z, self.devs = view, others, z, to_z, devs
        self.send, self.recv, self.tsend, self.trecv = sems

    def make(self, way, k, sender):
        sign = 1 if way == 0 else -1
        hops, owner = ((1, 0), (2, 0), (1, 2), (2, 2))[k]
        start = self.z if sender else self.z - sign * hops
        block = (start - sign * owner + 16) % 8
        part = self.view(block, way if k == 3 else None)
        return remote(
            part, part, self.send.at[way, k], self.recv.at[way, k],
            self.to_z((self.z + sign * hops + 8) % 8),
        )

    def pair(self, way, k, i, view):
        sign = 1 if way == 0 else -1
        block = (self.z - sign * (k + 1) + 16) % 8
        part = view(block, way if k == 3 else None)
        return remote(
            part, part, self.tsend.at[i, way, k], self.trecv.at[i, way, k], self.devs[i]
        )

    def start(self):
        for k in (1, 0):
            for way in (0, 1):
                self.make(way, k, True).start()

    def arrive(self, way, k):
        self.make(way, k, False).wait_recv()
        for i in (1, 2, 0):
            self.pair(way, k, i, self.view).start()

    def middle(self):
        for way in (0, 1):
            self.arrive(way, 1)
            self.make(way, 3, True).start()
            self.make(way, 2, True).start()
        for way in (0, 1):
            self.arrive(way, 0)

    def last(self):
        for k in (3, 2):
            for way in (0, 1):
                self.arrive(way, k)

    def twins(self):
        for k in range(4):
            for way in (0, 1):
                for i in range(3):
                    self.pair(way, k, i, self.others[i]).wait_recv()

    def drain(self):
        for k in range(4):
            for way in (0, 1):
                self.make(way, k, True).wait_send()
                for i in range(3):
                    self.pair(way, k, i, self.view).wait_send()


class Plane:
    def __init__(self, view, src, a, b, a_dev, b_dev, sems):
        self.view, self.src, self.a, self.b = view, src, a, b
        self.a_dev, self.b_dev = a_dev, b_dev
        self.sa, self.ra, self.sb, self.rb = sems
        self.drains = []

    def go(self, src, dst, send, recv, to):
        make = lambda: remote(src, dst, send, recv, to)
        make().start()
        self.drains.append(lambda: make().wait_send())

    def wait(self, dst, recv, to):
        remote(dst, dst, recv, recv, to).wait_recv()

    def near(self, at, way):
        return (at + (1 if way == 0 else 3)) % 4

    def entry(self, j):
        at = [self.a, self.near(self.a, 1), self.near(self.a, 0)] + [(self.a + 2) % 4] * 2
        return at[j], (None if j < 3 else j - 3)

    def send_a(self):
        own = self.view(self.a, self.b)
        for way in (0, 1):
            self.go(
                self.src, own, self.sa.at[0, way], self.ra.at[0, way],
                self.a_dev(self.near(self.a, way)),
            )

    def send_b(self, j, src=None):
        at, half = self.entry(j)
        part = self.view(at, self.b, half)
        for way in (0, 1):
            self.go(
                part if src is None else src, part, self.sb.at[0, way, j], self.rb.at[0, way, j],
                self.b_dev(self.near(self.b, way)),
            )

    def pass_a(self):
        for way in (0, 1):
            at = self.near(self.a, 1 - way)
            self.wait(self.view(at, self.b), self.ra.at[0, way], self.a_dev(at))
            half = self.view(at, self.b, way)
            self.go(
                half, half, self.sa.at[1, way], self.ra.at[1, way],
                self.a_dev(self.near(self.a, way)),
            )
            self.send_b(1 + way)

    def pass_far(self):
        far = (self.a + 2) % 4
        for way in (0, 1):
            self.wait(self.view(far, self.b, way), self.ra.at[1, way], self.a_dev(far))
            self.send_b(3 + way)

    def pass_b(self, j):
        at, half = self.entry(j)
        for way in (0, 1):
            near = self.near(self.b, 1 - way)
            self.wait(self.view(at, near, half), self.rb.at[0, way, j], self.b_dev(near))
            if half is None or half == way:
                part = self.view(at, near, way)
                self.go(
                    part, part, self.sb.at[1, way, j], self.rb.at[1, way, j],
                    self.b_dev(self.near(self.b, way)),
                )

    def end_b(self, j):
        at, half = self.entry(j)
        far = (self.b + 2) % 4
        for way in (0, 1):
            if half is None or half == way:
                self.wait(self.view(at, far, way), self.rb.at[1, way, j], self.b_dev(far))


class Twin:
    def __init__(self, ring, other, send, recv, dev):
        self.ring, self.other, self.sems, self.dev = ring, other, (send, recv), dev

    def make(self, way, step, half, view):
        part = view(self.ring.block(way, step + 1), half)
        return remote(
            part, part, self.sems[0].at[way, step, half], self.sems[1].at[way, step, half], self.dev
        )

    def __call__(self, way, step, half):
        self.make(way, step, half, self.ring.view).start()

    def each(self, steps):
        return [(way, step, half) for step in steps for way, half in self.ring.items(step)]

    def wait_recv(self, steps):
        for item in self.each(steps):
            self.make(*item, self.other).wait_recv()

    def drain(self):
        for item in self.each(range(4)):
            self.make(*item, self.ring.view).wait_send()


def rows_of(start, size, unit):
    return pl.ds(pl.multiple_of(start, unit), size)


def kernel(
    spans, lens, px, rx, gain, qg, kg, inv, wq, wkv, wo,
    both,
    xr, nb, wqb, wkb, wob, wkl, accq, acck, cosb, sinb, rpos, kpos, qb, kvp, kvr, atts, attb,
    osend, ry, xs, xrx,
    loc, xas, xar, xbs, xbr, gs, gr, ks, kr, qrs, qrr, krs, krr, ors, orr, ots, otr, o1,
    nbs, nbr, kvs, kvrv, vrs, vrr, vts, vtr, ats, atr, ys, yr, zs, zr,
):
    ctx, tp = lax.axis_index("ctx"), lax.axis_index("tp")
    low, z, c = ctx // 16, (ctx // 2) % 8, ctx % 2
    hi, y = tp // 4, tp % 4
    x = hi * 2 + low
    olow, oc = 1 - low, 1 - c

    def dev(low_, z_, c_, hi_, y_):
        return (low_ * 16 + z_ * 2 + c_, hi_ * 4 + y_)

    def at_x(x_):
        return dev(x_ % 2, z, c, x_ // 2, y)

    def at_y(y_):
        return dev(low, z, c, hi, y_)

    def at_g(low_, c_):
        return dev(low_, z, c_, hi, y)

    x_up, x_dn, x_far = (x + 1) % 4, (x + 3) % 4, (x + 2) % 4
    y_up, y_dn, y_far = (y + 1) % 4, (y + 3) % 4, (y + 2) % 4
    z_up = dev(low, (z + 1) % 8, c, hi, y)
    z_dn = dev(low, (z + 7) % 8, c, hi, y)
    twin = at_g(low, oc)
    group = [(low, oc), (olow, c), (olow, oc)]

    partners = [at_g(*m) for m in group] + [z_up, z_dn]
    partners += [at_y(y_up), at_y(y_dn), at_y(y_far)]
    partners += [dev(low, (z + 2) % 8, c, hi, y), dev(low, (z + 6) % 8, c, hi, y)]
    partners += [dev(low, z, c, 1 - hi, y), dev(olow, z, c, 1 - hi, y)]
    barrier = pltpu.get_barrier_semaphore()
    for partner in partners:
        pl.semaphore_signal(barrier, inc=1, device_id=partner, device_id_type=MESH)
    for kind in range(2):
        wkl[kind] = wkv[:, kind, :]
    pl.semaphore_wait(barrier, len(partners))

    drains = []

    def finish():
        for drain in drains:
            drain()

    def block_of(part, x_, y_, half=None):
        first, count = (0, 64) if half is None else (half * 32, 32)
        return xr.at[
            part, rows_of((x_ % 2) * 64 + first, count, 32),
            rows_of(((x_ // 2) * 4 + y_) * 640, 640, 128),
        ]

    prompts = Plane(
        lambda a, b, h=None: block_of(0, a, b, h), px, x, y, at_x, at_y,
        (xas.at[0], xar.at[0], xbs.at[0], xbr.at[0]),
    )
    answers = Plane(
        lambda a, b, h=None: block_of(1, b, a, h), rx, y, x, at_y, at_x,
        (xas.at[1], xar.at[1], xbs.at[1], xbr.at[1]),
    )
    planes = (prompts, answers)
    own0, own1 = block_of(0, x, y), block_of(1, x, y)

    group4 = [(low, c)] + group

    def piece(buf, z_, low_, c_):
        return buf.at[rows_of(low_ * 2560 + z_ * 320 + c_ * 160, 160, 32)]

    def wq_cols(low_, c_):
        return wq.at[:, rows_of((low_ * 2 + c_) * 256, 256, 256)]

    def wq_send(i):
        low_, c_ = group[i]
        return remote(
            wq_cols(low_, c_), piece(wqb, z, low, c), gs.at[i], gr.at[i], at_g(low_, c_)
        )

    def wk_cols(low_):
        return wkl.at[low_]

    def wk_send(i, low_):
        return remote(wk_cols(low_), piece(wkb, z, low, c), ks.at[i], kr.at[i], at_g(low_, 0))

    qring = Ring(
        lambda z_, p: piece(wqb, z_, *group4[p]), qrs, qrr, z, z_up, z_dn, 4
    )
    kring = Ring(
        lambda z_, p: piece(wkb, z_, *group4[p]), krs, krr, z, z_up, z_dn, 4
    )

    def if_keys(run):
        pl.when(c == 0)(run)

    prompts.send_a()
    prompts.send_b(0, px)

    @pl.when(c == 0)
    def _():
        kring.start(0, wk_cols(low))
        wk_send(1, olow).start()
        pltpu.make_async_copy(wk_cols(low), piece(wkb, z, low, c), loc.at[3]).start()

    @pl.when(c == 1)
    def _():
        wk_send(0, low).start()
        wk_send(2, olow).start()

    for i in range(3):
        wq_send(i).start()
    qring.start(0, wq_cols(low, c))
    answers.send_a()
    answers.send_b(0, rx)

    local0 = pltpu.make_async_copy(px, own0, loc.at[0])
    local1 = pltpu.make_async_copy(rx, own1, loc.at[1])
    local2 = pltpu.make_async_copy(wq_cols(low, c), piece(wqb, z, low, c), loc.at[2])
    local0.start()
    local1.start()
    local2.start()

    def wo_view(c_):
        return lambda z_, h: wob.at[rows_of(z_ * 320 + c_ * 160 + h * 80, 80, 16)]

    wo_own = wob.at[rows_of(z * 320 + c * 160, 160, 32)]
    local4 = pltpu.make_async_copy(wo, wo_own, loc.at[4])
    local4.start()

    oring = Ring(wo_view(c), ors, orr, z, z_up, z_dn)
    otwin = Twin(oring, wo_view(oc), ots, otr, twin)
    for h in range(2):
        oring.start(h, wo.at[pl.ds(h * 80, 80)])
    remote(wo, wo_own, o1.at[0], o1.at[1], twin).start()
    drains.append(lambda: remote(wo_own, wo_own, o1.at[0], o1.at[1], twin).wait_send())
    drains.append(oring.drain)
    drains.append(otwin.drain)

    @if_keys
    def _():
        for i in range(3):
            here = piece(wkb, z, *group[i])
            remote(here, here, ks.at[i], kr.at[i], twin).wait_recv()
            kring.start(i + 1)

    prompts.pass_a()
    prompts.pass_b(0)
    for i in range(3):
        here = piece(wqb, z, *group[i])
        remote(here, here, gs.at[i], gr.at[i], twin).wait_recv()
        qring.start(i + 1)
    prompts.pass_far()
    if_keys(lambda: kring.forward(1))
    answers.pass_a()
    qring.forward(1, parts=(0,))
    prompts.pass_b(1)
    prompts.pass_b(2)
    if_keys(lambda: kring.forward(2))
    prompts.pass_b(3)
    prompts.pass_b(4)
    answers.pass_b(0)
    answers.pass_far()
    qring.forward(1, parts=(1, 2, 3))
    if_keys(lambda: kring.forward(3))

    iota = lax.broadcasted_iota(jnp.int32, (32, 128), 0)
    for c_ in range(2):
        for low_ in range(2):
            for h in range(2):
                sid = spans[2 * (low_ * 16 + z * 2 + c_) + h]
                first = c_ * 128 + low_ * 64 + h * 32
                rpos[pl.ds(first, 32), :] = (sid * 32 + iota).astype(F32)
                rpos[pl.ds(256 + first, 32), :] = (2048 + c_ * 64 + h * 32 + iota).astype(F32)
    first_half = lax.broadcasted_iota(jnp.int32, (128, 128), 1) < 64

    @pl.loop(0, 4)
    def _(i):
        rows = rows_of(i * 128, 128, 128)
        angles = rpos[rows, :] * inv[...]
        cosb[rows, :] = jnp.cos(angles)
        sine = jnp.sin(angles)
        sinb[rows, :] = jnp.where(first_half, -sine, sine)

    for copy in (local0, local1, local2, local4):
        copy.wait()
    for j in range(5):
        prompts.end_b(j)

    drains.append(lambda: [drain() for plane in planes for drain in plane.drains])
    drains.append(qring.drain)
    drains.append(lambda: [wq_send(i).wait_send() for i in range(3)])

    def drain_keys():
        @pl.when(c == 0)
        def _():
            kring.drain()
            wk_send(1, olow).wait_send()

        @pl.when(c == 1)
        def _():
            wk_send(0, low).wait_send()
            wk_send(2, olow).wait_send()

    drains.append(drain_keys)

    def normed(c_, g):
        return nb.at[rows_of((g // 2) * 256 + c_ * 128 + (g % 2) * 64, 64, 64)]

    def norm_send(c_, g):
        return remote(normed(c_, g), normed(c_, g), nbs.at[g], nbr.at[g], twin)

    def norm(g):
        @pl.loop(0, 4)
        def _(i):
            rows = xr[g // 2, rows_of((g % 2) * 64 + i * 16, 16, 16), :].astype(F32)
            mean = jnp.mean(rows * rows, axis=-1, keepdims=True)
            first = (g // 2) * 256 + c * 128 + (g % 2) * 64 + i * 16
            nb[rows_of(first, 16, 16), :] = (
                rows * lax.rsqrt(mean + 1e-06) * gain[...]
            ).astype(BF)

        norm_send(c, g).start()

    drains.append(lambda: [norm_send(c, g).wait_send() for g in range(4)])
    norm(0)
    norm(1)
    if_keys(kring.last)
    if_keys(lambda: pltpu.make_async_copy(wk_cols(low), piece(wkb, z, low, c), loc.at[3]).wait())
    qring.forward(2, parts=(0,))
    for j in range(1, 5):
        answers.pass_b(j)
    for g in range(2):
        norm_send(oc, g).wait_recv()

    def head(values, gains, rows):
        mean = jnp.mean(values * values, axis=-1, keepdims=True)
        values = values * lax.rsqrt(mean + 1e-06) * gains[...]
        return values * cosb[rows, :] + pltpu.roll(values, 64, 1) * sinb[rows, :]

    def kv_send(i, p):
        low_, c_ = group[i]
        own = kvp.at[low, rows_of(z * 256, 256, 256)] if p == 0 else kvr.at[low]
        return remote(
            own, own, kvs.at[i, p], kvrv.at[0 if i == 0 else 1, p], at_g(low_, c_)
        )

    def keys(p):
        rows = pl.ds(p * 256, 256)
        acck[rows, :] = jnp.zeros((256, 128), F32)

        @pl.loop(0, 10)
        def _(i):
            part = rows_of(i * 512, 512, 512)
            acck[rows, :] += jnp.dot(nb[rows, part], wkb[part, :], preferred_element_type=F32)

        raw = acck[rows, :]
        mine = jnp.where(low == 0, head(raw, kg, rows), raw).astype(BF)
        if p == 0:
            kvp[low, rows_of(z * 256, 256, 256), :] = mine
        else:
            kvr[low] = mine
        for k in (1, 2, 0):
            kv_send(k, p).start()

    if_keys(lambda: keys(0))
    qring.forward(2, parts=(1, 2, 3))
    for j in range(5):
        answers.end_b(j)
    norm(2)
    norm(3)

    def drain_kv():
        @pl.when(c == 0)
        def _():
            for p in range(2):
                for i in range(3):
                    kv_send(i, p).wait_send()

    drains.append(drain_kv)

    def kv_wait(kind, i, p):
        part = kvp.at[kind, rows_of(z * 256, 256, 256)] if p == 0 else kvr.at[kind]
        remote(part, part, kvs.at[0, p], kvrv.at[i, p], twin).wait_recv()

    lane = lax.broadcasted_iota(jnp.int32, (8, 2048), 1)

    def key_positions(j, held):
        z_, c_, low_, h = j // 8, (j // 4) % 2, (j // 2) % 2, j % 2
        sid = spans[2 * (low_ * 16 + z_ * 2 + c_) + h]
        return jnp.where(lane // 32 == j, sid * 32 + lane % 32, held)

    kpos[...] = lax.fori_loop(
        0, 64, key_positions, jnp.zeros((8, 2048), jnp.int32)
    ).astype(F32)
    pl.when(c == 1)(lambda: kv_wait(low, 0, 0))
    kv_wait(olow, 1, 0)

    def kv_view(low_, kind):
        def view(z_, h):
            first, count = (0, 128) if h is None else (h * 64, 64)
            return kvp.at[kind, rows_of(z_ * 256 + low_ * 128 + first, count, 64)]

        return view

    spread = Spread(
        kv_view(low, c), [kv_view(*m) for m in group], (vrs, vrr, vts, vtr), z,
        lambda z_: dev(low, z_, c, hi, y), [at_g(*m) for m in group],
    )
    spread.start()
    drains.append(spread.drain)
    qring.forward(3)
    for g in (2, 3):
        norm_send(oc, g).wait_recv()
    spread.middle()
    oring.forward(1, otwin, (0,))
    oring.forward(1, otwin, (1,))
    if_keys(lambda: keys(1))
    qring.last()
    spread.last()
    accq[...] = jnp.zeros_like(accq)

    @pl.loop(0, 10)
    def _(i):
        part = rows_of(i * 512, 512, 512)
        accq[...] += jnp.dot(nb[:, part], wqb[part, :], preferred_element_type=F32)

    oring.forward(2, otwin, (0,))
    for i in range(4):
        rows = pl.ds(i * 128, 128)
        for h in range(2):
            qb[i, pl.ds(h * 128, 128), :] = head(
                accq[rows, pl.ds(h * 128, 128)], qg, rows
            ).astype(BF)
    pl.when(c == 1)(lambda: kv_wait(low, 0, 1))
    kv_wait(olow, 1, 1)
    spread.twins()

    scale = 128 ** (-0.5)

    def attend(c_, p):
        queries = qb[p * 2 + c_]
        scores = lax.dot_general(queries, kvp[0], NT, preferred_element_type=F32) * scale
        if p == 0:
            mine = rpos[rows_of(c_ * 128, 128, 128), :][:, :1]
            allowed = kpos[:1, :] <= jnp.concatenate([mine, mine], axis=0)
            scores = jnp.where(allowed, scores, -1e30)
        peak = jnp.max(scores, axis=-1, keepdims=True)
        if p == 1:
            own = lax.dot_general(queries, kvr[0], NT, preferred_element_type=F32) * scale
            q_row = lax.broadcasted_iota(jnp.int32, (256, 256), 0) % 128
            k_row = lax.broadcasted_iota(jnp.int32, (256, 256), 1)
            allowed = ((q_row // 64) == ((k_row // 64) % 2)) & (
                (k_row // 128) * 64 + k_row % 64 <= c_ * 64 + q_row % 64
            )
            own = jnp.where(allowed, own, -1e30)
            peak = jnp.maximum(peak, jnp.max(own, axis=-1, keepdims=True))
        weights = jnp.exp(scores - peak)
        total = jnp.sum(weights, axis=-1, keepdims=True)
        summed = jnp.dot(weights.astype(BF), kvp[1], preferred_element_type=F32)
        if p == 1:
            more = jnp.exp(own - peak)
            total = total + jnp.sum(more, axis=-1, keepdims=True)
            summed = summed + jnp.dot(more.astype(BF), kvr[1], preferred_element_type=F32)
        result = (summed / total).astype(BF)
        for h in range(2):
            atts[c_, pl.ds(p * 128, 128), pl.ds(h * 128, 128)] = result[h * 128 : (h + 1) * 128]

    def att_cols(low_, c_):
        return attb.at[:, rows_of((low_ * 2 + c_) * 256, 256, 256)]

    def att_send(i):
        low_, c_ = group[i]
        return remote(atts.at[c_], att_cols(low, c), ats.at[i], atr.at[i], at_g(low_, c_))

    oring.forward(2, otwin, (1,))
    attend(oc, 0)
    attend(oc, 1)
    att_send(2).start()
    att_send(0).start()
    attend(c, 0)
    attend(c, 1)
    att_send(1).start()
    oring.forward(3, otwin)
    drains.append(lambda: [att_send(i).wait_send() for i in range(3)])
    attb[:, rows_of((low * 2 + c) * 256, 256, 256)] = atts[c]
    other_own = wob.at[rows_of(z * 320 + oc * 160, 160, 32)]
    remote(other_own, other_own, o1.at[0], o1.at[1], twin).wait_recv()
    otwin.wait_recv(range(2))
    for i in range(3):
        part = att_cols(*group[i])
        remote(part, part, ats.at[i], atr.at[i], twin).wait_recv()

    early, late = (1 - z % 2) * 384, (z % 2) * 256

    def cols_of(k):
        return pl.ds(0, 640) if k < 3 else (
            rows_of(early, 256, 128) if k == 3 else rows_of(late, 384, 128)
        )

    def y_send(k, p, y_):
        place = (y_ - y + 3) % 4
        rows, cols = pl.ds(p * 128, 128), cols_of(k)
        return remote(
            osend.at[min(k, 3), rows, cols], ry.at[place, rows, cols],
            ys.at[k, p], yr.at[place, p, k // 4], at_y(y_),
        )

    def y_of(k):
        return (z // 2 + (0, 3 + 2 * (z % 2), 5 - 2 * (z % 2), 2, 2)[k]) % 4

    def project(k):
        y_ = y_of(k)
        first = y_ * 640 + (0, 0, 0, early, late)[k]
        weights = wob[rows_of(first, (640, 640, 640, 256, 384)[k], 128), :]
        osend[min(k, 3), :, cols_of(k)] = lax.dot_general(
            attb[...], weights, NT, preferred_element_type=F32
        ).astype(BF)
        for p in range(2):
            pl.when(y_ != y)(lambda p=p: y_send(k, p, y_).start())

    def drain_y():
        for k in range(5):
            for p in range(2):
                pl.when(y_of(k) != y)(lambda k=k, p=p: y_send(k, p, y_of(k)).wait_send())

    drains.append(drain_y)
    project(0)
    project(1)
    otwin.wait_recv((2,))
    project(2)
    project(3)
    oring.last(otwin)
    otwin.wait_recv((3,))
    project(4)

    def x_send(low_, p):
        return remote(
            xs.at[pl.ds(p * 128 + low_ * 64, 64)], xrx.at[hi, p],
            zs.at[low_, p], zr.at[hi, p], dev(low_, z, c, low, y),
        )

    mine = (y - z // 2 + 4) % 4
    slot = jnp.where(mine == 2, 3, jnp.where(mine % 2 == 0, 0, 2 - (mine // 2 + z) % 2))
    for p in range(2):
        rows = pl.ds(p * 128, 128)

        def y_wait(k, p=p):
            for i in range(3):
                part = ry.at[i, pl.ds(p * 128, 128), cols_of(k)]
                remote(part, part, ys.at[0, p], yr.at[i, p, k // 4], twin).wait_recv()

        @pl.when(mine == 2)
        def _(y_wait=y_wait):
            y_wait(3)
            y_wait(4)

        pl.when(mine != 2)(lambda: y_wait(0))
        total = osend[slot, rows, :].astype(F32)
        for i in range(3):
            total += ry[i, rows, :].astype(F32)
        xs[rows, :] = total.astype(BF)
        for low_ in range(2):
            here = jnp.logical_and(hi == low, low == low_)

            @pl.when(here)
            def _(low_=low_, p=p):
                xrx[hi, p] = xs[pl.ds(p * 128 + low_ * 64, 64), :]

            pl.when(jnp.logical_not(here))(lambda low_=low_, p=p: x_send(low_, p).start())

    offsets = c * 64 + lax.broadcasted_iota(jnp.int32, (64, 640), 0)
    for p in range(2):
        for hi_ in range(2):

            @pl.when(jnp.logical_not(jnp.logical_and(hi == low, hi == hi_)))
            def _(hi_=hi_, p=p):
                part = xrx.at[hi_, p]
                remote(part, part, zs.at[0, p], zr.at[hi_, p], twin).wait_recv()

        total = xrx[0, p].astype(F32) + xrx[1, p].astype(F32)
        if p == 0:
            both[pl.ds(0, 64), :] = total.astype(BF)
        else:
            both[pl.ds(64, 64), :] = jnp.where(offsets < lens[ctx // 2], total, 0.0).astype(BF)

    finish()
    for low_ in range(2):
        here = jnp.logical_and(hi == low, low == low_)

        @pl.when(jnp.logical_not(here))
        def _(low_=low_):
            for p in range(2):
                x_send(low_, p).wait_send()


def body(prompt_x, resp_x, span_ids, lengths, in_gain, q_gain, k_gain, w_query, w_keyval, w_out):
    half = 1000000.0 ** (-(np.arange(64) * 2.0) / 128)
    inverse = np.concatenate([half, half])[None, :].astype(np.float32)
    dma = pltpu.SemaphoreType.DMA
    hbm, vmem, smem = (pl.BlockSpec(memory_space=s) for s in (pl.ANY, pltpu.VMEM, pltpu.SMEM))
    out = jax.ShapeDtypeStruct((128, 640), BF)
    both = pl.pallas_call(
        kernel,
        out_shape=out,
        in_specs=[smem, smem, hbm, hbm, vmem, vmem, vmem, vmem, hbm, vmem, hbm],
        out_specs=vmem,
        scratch_shapes=[
            pltpu.VMEM((2, 128, 5120), BF),
            pltpu.VMEM((512, 5120), BF),
            pltpu.VMEM((5120, 256), BF),
            pltpu.VMEM((5120, 128), BF),
            pltpu.VMEM((2560, 1024), BF),
            pltpu.VMEM((2, 160, 128), BF),
            pltpu.VMEM((512, 256), F32),
            pltpu.VMEM((512, 128), F32),
            pltpu.VMEM((512, 128), F32),
            pltpu.VMEM((512, 128), F32),
            pltpu.VMEM((512, 128), F32),
            pltpu.VMEM((8, 2048), F32),
            pltpu.VMEM((4, 256, 128), BF),
            pltpu.VMEM((2, 2048, 128), BF),
            pltpu.VMEM((2, 256, 128), BF),
            pltpu.VMEM((2, 256, 256), BF),
            pltpu.VMEM((256, 1024), BF),
            pltpu.VMEM((4, 256, 640), BF),
            pltpu.VMEM((3, 256, 640), BF),
            pltpu.VMEM((256, 640), BF),
            pltpu.VMEM((2, 2, 64, 640), BF),
            dma((5,)),
            dma((2, 2, 2)), dma((2, 2, 2)),
            dma((2, 2, 2, 5)), dma((2, 2, 2, 5)),
            dma((3,)), dma((3,)),
            dma((3,)), dma((3,)),
            dma((2, 4, 4)), dma((2, 4, 4)),
            dma((2, 4, 4)), dma((2, 4, 4)),
            dma((2, 4, 2)), dma((2, 4, 2)),
            dma((2, 4, 2)), dma((2, 4, 2)),
            dma((2,)),
            dma((4,)), dma((4,)),
            dma((3, 2)), dma((2, 2)),
            dma((2, 4)), dma((2, 4)),
            dma((3, 2, 4)), dma((3, 2, 4)),
            dma((3,)), dma((3,)),
            dma((5, 2)), dma((3, 2, 2)),
            dma((2, 2)), dma((2, 2)),
        ],
        compiler_params=pltpu.CompilerParams(
            collective_id=0, has_side_effects=True, vmem_limit_bytes=56 * 2**20
        ),
        name="attention_block",
    )(
        span_ids, lengths, prompt_x, resp_x, in_gain[None, :], q_gain[None, :], k_gain[None, :],
        inverse, w_query, w_keyval, jnp.transpose(w_out),
    )
    return both[:64], both[64:]


def solution(mesh):
    placed = (
        P("ctx", "tp"),
        P("ctx", "tp"),
        P(),
        P(),
        P(),
        P(),
        P(),
        P("ctx", "tp"),
        P("ctx", None, "tp"),
        P("tp", "ctx"),
    )
    return jax.shard_map(
        body,
        mesh=mesh,
        in_specs=placed,
        out_specs=(P("ctx", "tp"), P("ctx", "tp")),
        check_vma=False,
    )
```

```python
import functools

import jax
import jax.numpy as jnp
import numpy as np
from jax import lax
from jax.experimental import pallas as pl
from jax.experimental.pallas import tpu as pltpu
from jax.sharding import PartitionSpec as P

MESH = pl.DeviceIdType.MESH
BF = jnp.bfloat16
F32 = jnp.float32
NT = (((1,), (1,)), ((), ()))


def remote(src, dst, send, recv, dev):
    return pltpu.make_async_remote_copy(
        src_ref=src, dst_ref=dst, send_sem=send, recv_sem=recv, device_id=dev, device_id_type=MESH
    )


class Ring:
    def __init__(self, view, send, recv, z, up_dev, down_dev, parts=2):
        self.view, self.send, self.recv, self.z, self.parts = view, send, recv, z, parts
        self.devs = (up_dev, down_dev)

    def items(self, step):
        every = [(way, part) for part in range(self.parts) for way in (0, 1)]
        return every if step < 3 else [i for i in every if i[0] == i[1] * 2 // self.parts]

    def block(self, way, step):
        return lax.rem(self.z + (8 - step if way == 0 else step), 8)

    def copy(self, way, step, part, src=None):
        there = self.view(self.block(way, step), part)
        return remote(
            there if src is None else src, there,
            self.send.at[way, step, part], self.recv.at[way, step, part], self.devs[way],
        )

    def arrived(self, way, step, part):
        here = self.view(self.block(way, step + 1), part)
        remote(
            here, here, self.send.at[way, step, part], self.recv.at[way, step, part],
            self.devs[way],
        ).wait_recv()

    def start(self, part, src=None):
        for way in (0, 1):
            self.copy(way, 0, part, src).start()

    def forward(self, step, then=None, parts=None):
        for way, part in self.items(step - 1):
            if parts is not None and part not in parts:
                continue
            self.arrived(way, step - 1, part)
            if step < 4 and (way, part) in self.items(step):
                self.copy(way, step, part).start()
            if then is not None:
                then(way, step - 1, part)

    def last(self, then=None):
        self.forward(4, then)

    def drain(self):
        for step in range(4):
            for way, part in self.items(step):
                self.copy(way, step, part).wait_send()


class Plane:
    def __init__(self, view, src, a, b, a_dev, b_dev, sems):
        self.view, self.src, self.a, self.b = view, src, a, b
        self.a_dev, self.b_dev = a_dev, b_dev
        self.sa, self.ra, self.sb, self.rb = sems
        self.drains = []

    def go(self, src, dst, send, recv, to):
        make = lambda: remote(src, dst, send, recv, to)
        make().start()
        self.drains.append(lambda: make().wait_send())

    def wait(self, dst, recv, to):
        remote(dst, dst, recv, recv, to).wait_recv()

    def near(self, at, way):
        return (at + (1 if way == 0 else 3)) % 4

    def entry(self, j):
        at = [self.a, self.near(self.a, 1), self.near(self.a, 0)] + [(self.a + 2) % 4] * 2
        return at[j], (None if j < 3 else j - 3)

    def send_a(self):
        own = self.view(self.a, self.b)
        for way in (0, 1):
            self.go(
                self.src, own, self.sa.at[0, way], self.ra.at[0, way],
                self.a_dev(self.near(self.a, way)),
            )

    def send_b(self, j, src=None):
        at, half = self.entry(j)
        part = self.view(at, self.b, half)
        for way in (0, 1):
            self.go(
                part if src is None else src, part, self.sb.at[0, way, j], self.rb.at[0, way, j],
                self.b_dev(self.near(self.b, way)),
            )

    def pass_a(self):
        for way in (0, 1):
            at = self.near(self.a, 1 - way)
            self.wait(self.view(at, self.b), self.ra.at[0, way], self.a_dev(at))
            half = self.view(at, self.b, way)
            self.go(
                half, half, self.sa.at[1, way], self.ra.at[1, way],
                self.a_dev(self.near(self.a, way)),
            )
            self.send_b(1 + way)

    def pass_far(self):
        far = (self.a + 2) % 4
        for way in (0, 1):
            self.wait(self.view(far, self.b, way), self.ra.at[1, way], self.a_dev(far))
            self.send_b(3 + way)

    def pass_b(self, j):
        at, half = self.entry(j)
        for way in (0, 1):
            near = self.near(self.b, 1 - way)
            self.wait(self.view(at, near, half), self.rb.at[0, way, j], self.b_dev(near))
            if half is None or half == way:
                part = self.view(at, near, way)
                self.go(
                    part, part, self.sb.at[1, way, j], self.rb.at[1, way, j],
                    self.b_dev(self.near(self.b, way)),
                )

    def end_b(self, j):
        at, half = self.entry(j)
        far = (self.b + 2) % 4
        for way in (0, 1):
            if half is None or half == way:
                self.wait(self.view(at, far, way), self.rb.at[1, way, j], self.b_dev(far))


class Spread:
    def __init__(self, view, others, sems, z, to_z, devs):
        self.view, self.others, self.z, self.to_z, self.devs = view, others, z, to_z, devs
        self.send, self.recv, self.tsend, self.trecv = sems

    def make(self, way, k, sender):
        sign = 1 if way == 0 else -1
        hops, owner = ((1, 0), (2, 0), (1, 2), (2, 2))[k]
        start = self.z if sender else self.z - sign * hops
        block = (start - sign * owner + 16) % 8
        part = self.view(block, way if k == 3 else None)
        return remote(
            part, part, self.send.at[way, k], self.recv.at[way, k],
            self.to_z((self.z + sign * hops + 8) % 8),
        )

    def pair(self, way, k, i, view):
        sign = 1 if way == 0 else -1
        block = (self.z - sign * (k + 1) + 16) % 8
        part = view(block, way if k == 3 else None)
        return remote(
            part, part, self.tsend.at[i, way, k], self.trecv.at[i, way, k], self.devs[i]
        )

    def start(self):
        for k in (1, 0):
            for way in (0, 1):
                self.make(way, k, True).start()

    def arrive(self, way, k):
        self.make(way, k, False).wait_recv()
        for i in (1, 2, 0):
            self.pair(way, k, i, self.view).start()

    def middle(self):
        for way in (0, 1):
            self.arrive(way, 1)
            self.make(way, 3, True).start()
            self.make(way, 2, True).start()
        for way in (0, 1):
            self.arrive(way, 0)

    def last(self):
        for k in (3, 2):
            for way in (0, 1):
                self.arrive(way, k)

    def twins(self):
        for k in range(4):
            for way in (0, 1):
                for i in range(3):
                    self.pair(way, k, i, self.others[i]).wait_recv()

    def drain(self):
        for k in range(4):
            for way in (0, 1):
                self.make(way, k, True).wait_send()
                for i in range(3):
                    self.pair(way, k, i, self.view).wait_send()


class Plane:
    def __init__(self, view, src, a, b, a_dev, b_dev, sems):
        self.view, self.src, self.a, self.b = view, src, a, b
        self.a_dev, self.b_dev = a_dev, b_dev
        self.sa, self.ra, self.sb, self.rb = sems
        self.drains = []

    def go(self, src, dst, send, recv, to):
        make = lambda: remote(src, dst, send, recv, to)
        make().start()
        self.drains.append(lambda: make().wait_send())

    def wait(self, dst, recv, to):
        remote(dst, dst, recv, recv, to).wait_recv()

    def near(self, at, way):
        return (at + (1 if way == 0 else 3)) % 4

    def entry(self, j):
        at = [self.a, self.near(self.a, 1), self.near(self.a, 0)] + [(self.a + 2) % 4] * 2
        return at[j], (None if j < 3 else j - 3)

    def send_a(self):
        own = self.view(self.a, self.b)
        for way in (0, 1):
            self.go(
                self.src, own, self.sa.at[0, way], self.ra.at[0, way],
                self.a_dev(self.near(self.a, way)),
            )

    def send_b(self, j, src=None):
        at, half = self.entry(j)
        part = self.view(at, self.b, half)
        for way in (0, 1):
            self.go(
                part if src is None else src, part, self.sb.at[0, way, j], self.rb.at[0, way, j],
                self.b_dev(self.near(self.b, way)),
            )

    def pass_a(self):
        for way in (0, 1):
            at = self.near(self.a, 1 - way)
            self.wait(self.view(at, self.b), self.ra.at[0, way], self.a_dev(at))
            half = self.view(at, self.b, way)
            self.go(
                half, half, self.sa.at[1, way], self.ra.at[1, way],
                self.a_dev(self.near(self.a, way)),
            )
            self.send_b(1 + way)

    def pass_far(self):
        far = (self.a + 2) % 4
        for way in (0, 1):
            self.wait(self.view(far, self.b, way), self.ra.at[1, way], self.a_dev(far))
            self.send_b(3 + way)

    def pass_b(self, j):
        at, half = self.entry(j)
        for way in (0, 1):
            near = self.near(self.b, 1 - way)
            self.wait(self.view(at, near, half), self.rb.at[0, way, j], self.b_dev(near))
            if half is None or half == way:
                part = self.view(at, near, way)
                self.go(
                    part, part, self.sb.at[1, way, j], self.rb.at[1, way, j],
                    self.b_dev(self.near(self.b, way)),
                )

    def end_b(self, j):
        at, half = self.entry(j)
        far = (self.b + 2) % 4
        for way in (0, 1):
            if half is None or half == way:
                self.wait(self.view(at, far, way), self.rb.at[1, way, j], self.b_dev(far))


class Twin:
    def __init__(self, ring, other, send, recv, dev):
        self.ring, self.other, self.sems, self.dev = ring, other, (send, recv), dev

    def make(self, way, step, half, view):
        part = view(self.ring.block(way, step + 1), half)
        return remote(
            part, part, self.sems[0].at[way, step, half], self.sems[1].at[way, step, half], self.dev
        )

    def __call__(self, way, step, half):
        self.make(way, step, half, self.ring.view).start()

    def each(self, steps):
        return [(way, step, half) for step in steps for way, half in self.ring.items(step)]

    def wait_recv(self, steps):
        for item in self.each(steps):
            self.make(*item, self.other).wait_recv()

    def drain(self):
        for item in self.each(range(4)):
            self.make(*item, self.ring.view).wait_send()


def rows_of(start, size, unit):
    return pl.ds(pl.multiple_of(start, unit), size)


def kernel(
    spans, lens, px, rx, gain, qg, kg, inv, wq, wkv, wo,
    both,
    xr, nb, wqb, wkb, wob, wkl, accq, acck, cosb, sinb, rpos, kpos, qb, kvp, kvr, atts, attb,
    osend, ry, xs, xrx,
    loc, xas, xar, xbs, xbr, gs, gr, ks, kr, qrs, qrr, krs, krr, ors, orr, ots, otr, o1,
    nbs, nbr, kvs, kvrv, vrs, vrr, vts, vtr, ats, atr, ys, yr, zs, zr,
):
    ctx, tp = lax.axis_index("ctx"), lax.axis_index("tp")
    low, z, c = ctx // 16, (ctx // 2) % 8, ctx % 2
    hi, y = tp // 4, tp % 4
    x = hi * 2 + low
    olow, oc = 1 - low, 1 - c

    def dev(low_, z_, c_, hi_, y_):
        return (low_ * 16 + z_ * 2 + c_, hi_ * 4 + y_)

    def at_x(x_):
        return dev(x_ % 2, z, c, x_ // 2, y)

    def at_y(y_):
        return dev(low, z, c, hi, y_)

    def at_g(low_, c_):
        return dev(low_, z, c_, hi, y)

    x_up, x_dn, x_far = (x + 1) % 4, (x + 3) % 4, (x + 2) % 4
    y_up, y_dn, y_far = (y + 1) % 4, (y + 3) % 4, (y + 2) % 4
    z_up = dev(low, (z + 1) % 8, c, hi, y)
    z_dn = dev(low, (z + 7) % 8, c, hi, y)
    twin = at_g(low, oc)
    group = [(low, oc), (olow, c), (olow, oc)]

    partners = [at_g(*m) for m in group] + [z_up, z_dn]
    partners += [at_y(y_up), at_y(y_dn), at_y(y_far)]
    partners += [dev(low, (z + 2) % 8, c, hi, y), dev(low, (z + 6) % 8, c, hi, y)]
    partners += [dev(low, z, c, 1 - hi, y), dev(olow, z, c, 1 - hi, y)]
    barrier = pltpu.get_barrier_semaphore()
    for partner in partners:
        pl.semaphore_signal(barrier, inc=1, device_id=partner, device_id_type=MESH)
    for kind in range(2):
        wkl[kind] = wkv[:, kind, :]
    pl.semaphore_wait(barrier, len(partners))

    drains = []

    def finish():
        for drain in drains:
            drain()

    def block_of(part, x_, y_, half=None):
        first, count = (0, 64) if half is None else (half * 32, 32)
        return xr.at[
            part, rows_of((x_ % 2) * 64 + first, count, 32),
            rows_of(((x_ // 2) * 4 + y_) * 640, 640, 128),
        ]

    prompts = Plane(
        lambda a, b, h=None: block_of(0, a, b, h), px, x, y, at_x, at_y,
        (xas.at[0], xar.at[0], xbs.at[0], xbr.at[0]),
    )
    answers = Plane(
        lambda a, b, h=None: block_of(1, b, a, h), rx, y, x, at_y, at_x,
        (xas.at[1], xar.at[1], xbs.at[1], xbr.at[1]),
    )
    planes = (prompts, answers)
    own0, own1 = block_of(0, x, y), block_of(1, x, y)

    group4 = [(low, c)] + group

    def piece(buf, z_, low_, c_):
        return buf.at[rows_of(low_ * 2560 + z_ * 320 + c_ * 160, 160, 32)]

    def wq_cols(low_, c_):
        return wq.at[:, rows_of((low_ * 2 + c_) * 256, 256, 256)]

    def wq_send(i):
        low_, c_ = group[i]
        return remote(
            wq_cols(low_, c_), piece(wqb, z, low, c), gs.at[i], gr.at[i], at_g(low_, c_)
        )

    def wk_cols(low_):
        return wkl.at[low_]

    def wk_send(i, low_):
        return remote(wk_cols(low_), piece(wkb, z, low, c), ks.at[i], kr.at[i], at_g(low_, 0))

    qring = Ring(
        lambda z_, p: piece(wqb, z_, *group4[p]), qrs, qrr, z, z_up, z_dn, 4
    )
    kring = Ring(
        lambda z_, p: piece(wkb, z_, *group4[p]), krs, krr, z, z_up, z_dn, 4
    )

    def if_keys(run):
        pl.when(c == 0)(run)

    prompts.send_a()
    prompts.send_b(0, px)

    @pl.when(c == 0)
    def _():
        kring.start(0, wk_cols(low))
        wk_send(1, olow).start()
        pltpu.make_async_copy(wk_cols(low), piece(wkb, z, low, c), loc.at[3]).start()

    @pl.when(c == 1)
    def _():
        wk_send(0, low).start()
        wk_send(2, olow).start()

    for i in range(3):
        wq_send(i).start()
    qring.start(0, wq_cols(low, c))
    answers.send_a()
    answers.send_b(0, rx)

    local0 = pltpu.make_async_copy(px, own0, loc.at[0])
    local1 = pltpu.make_async_copy(rx, own1, loc.at[1])
    local2 = pltpu.make_async_copy(wq_cols(low, c), piece(wqb, z, low, c), loc.at[2])
    local0.start()
    local1.start()
    local2.start()

    def wo_view(c_):
        return lambda z_, h: wob.at[rows_of(z_ * 320 + c_ * 160 + h * 80, 80, 16)]

    wo_own = wob.at[rows_of(z * 320 + c * 160, 160, 32)]
    local4 = pltpu.make_async_copy(wo, wo_own, loc.at[4])
    local4.start()

    oring = Ring(wo_view(c), ors, orr, z, z_up, z_dn)
    otwin = Twin(oring, wo_view(oc), ots, otr, twin)
    for h in range(2):
        oring.start(h, wo.at[pl.ds(h * 80, 80)])
    remote(wo, wo_own, o1.at[0], o1.at[1], twin).start()
    drains.append(lambda: remote(wo_own, wo_own, o1.at[0], o1.at[1], twin).wait_send())
    drains.append(oring.drain)
    drains.append(otwin.drain)

    @if_keys
    def _():
        for i in range(3):
            here = piece(wkb, z, *group[i])
            remote(here, here, ks.at[i], kr.at[i], twin).wait_recv()
            kring.start(i + 1)

    prompts.pass_a()
    prompts.pass_b(0)
    for i in range(3):
        here = piece(wqb, z, *group[i])
        remote(here, here, gs.at[i], gr.at[i], twin).wait_recv()
        qring.start(i + 1)
    prompts.pass_far()
    if_keys(lambda: kring.forward(1))
    answers.pass_a()
    qring.forward(1, parts=(0,))
    prompts.pass_b(1)
    prompts.pass_b(2)
    if_keys(lambda: kring.forward(2))
    prompts.pass_b(3)
    prompts.pass_b(4)
    answers.pass_b(0)
    answers.pass_far()
    qring.forward(1, parts=(1, 2, 3))
    if_keys(lambda: kring.forward(3))

    iota = lax.broadcasted_iota(jnp.int32, (32, 128), 0)
    for c_ in range(2):
        for low_ in range(2):
            for h in range(2):
                sid = spans[2 * (low_ * 16 + z * 2 + c_) + h]
                first = c_ * 128 + low_ * 64 + h * 32
                rpos[pl.ds(first, 32), :] = (sid * 32 + iota).astype(F32)
                rpos[pl.ds(256 + first, 32), :] = (2048 + c_ * 64 + h * 32 + iota).astype(F32)
    first_half = lax.broadcasted_iota(jnp.int32, (128, 128), 1) < 64

    @pl.loop(0, 4)
    def _(i):
        rows = rows_of(i * 128, 128, 128)
        angles = rpos[rows, :] * inv[...]
        cosb[rows, :] = jnp.cos(angles)
        sine = jnp.sin(angles)
        sinb[rows, :] = jnp.where(first_half, -sine, sine)

    for copy in (local0, local1, local2, local4):
        copy.wait()
    for j in range(5):
        prompts.end_b(j)

    drains.append(lambda: [drain() for plane in planes for drain in plane.drains])
    drains.append(qring.drain)
    drains.append(lambda: [wq_send(i).wait_send() for i in range(3)])

    def drain_keys():
        @pl.when(c == 0)
        def _():
            kring.drain()
            wk_send(1, olow).wait_send()

        @pl.when(c == 1)
        def _():
            wk_send(0, low).wait_send()
            wk_send(2, olow).wait_send()

    drains.append(drain_keys)

    def normed(c_, g):
        return nb.at[rows_of((g // 2) * 256 + c_ * 128 + (g % 2) * 64, 64, 64)]

    def norm_send(c_, g):
        return remote(normed(c_, g), normed(c_, g), nbs.at[g], nbr.at[g], twin)

    def norm(g):
        @pl.loop(0, 4)
        def _(i):
            rows = xr[g // 2, rows_of((g % 2) * 64 + i * 16, 16, 16), :].astype(F32)
            mean = jnp.mean(rows * rows, axis=-1, keepdims=True)
            first = (g // 2) * 256 + c * 128 + (g % 2) * 64 + i * 16
            nb[rows_of(first, 16, 16), :] = (
                rows * lax.rsqrt(mean + 1e-06) * gain[...]
            ).astype(BF)

        norm_send(c, g).start()

    drains.append(lambda: [norm_send(c, g).wait_send() for g in range(4)])
    norm(0)
    norm(1)
    if_keys(kring.last)
    if_keys(lambda: pltpu.make_async_copy(wk_cols(low), piece(wkb, z, low, c), loc.at[3]).wait())
    qring.forward(2, parts=(0,))
    for j in range(1, 5):
        answers.pass_b(j)
    for g in range(2):
        norm_send(oc, g).wait_recv()

    def head(values, gains, rows):
        mean = jnp.mean(values * values, axis=-1, keepdims=True)
        values = values * lax.rsqrt(mean + 1e-06) * gains[...]
        return values * cosb[rows, :] + pltpu.roll(values, 64, 1) * sinb[rows, :]

    def kv_send(i, p):
        low_, c_ = group[i]
        own = kvp.at[low, rows_of(z * 256, 256, 256)] if p == 0 else kvr.at[low]
        return remote(
            own, own, kvs.at[i, p], kvrv.at[0 if i == 0 else 1, p], at_g(low_, c_)
        )

    def keys(p):
        rows = pl.ds(p * 256, 256)
        acck[rows, :] = jnp.zeros((256, 128), F32)

        @pl.loop(0, 10)
        def _(i):
            part = rows_of(i * 512, 512, 512)
            acck[rows, :] += jnp.dot(nb[rows, part], wkb[part, :], preferred_element_type=F32)

        raw = acck[rows, :]
        mine = jnp.where(low == 0, head(raw, kg, rows), raw).astype(BF)
        if p == 0:
            kvp[low, rows_of(z * 256, 256, 256), :] = mine
        else:
            kvr[low] = mine
        for k in (1, 2, 0):
            kv_send(k, p).start()

    if_keys(lambda: keys(0))
    qring.forward(2, parts=(1, 2, 3))
    for j in range(5):
        answers.end_b(j)
    norm(2)
    norm(3)

    def drain_kv():
        @pl.when(c == 0)
        def _():
            for p in range(2):
                for i in range(3):
                    kv_send(i, p).wait_send()

    drains.append(drain_kv)

    def kv_wait(kind, i, p):
        part = kvp.at[kind, rows_of(z * 256, 256, 256)] if p == 0 else kvr.at[kind]
        remote(part, part, kvs.at[0, p], kvrv.at[i, p], twin).wait_recv()

    pl.when(c == 1)(lambda: kv_wait(low, 0, 0))
    kv_wait(olow, 1, 0)

    def kv_view(low_, kind):
        def view(z_, h):
            first, count = (0, 128) if h is None else (h * 64, 64)
            return kvp.at[kind, rows_of(z_ * 256 + low_ * 128 + first, count, 64)]

        return view

    spread = Spread(
        kv_view(low, c), [kv_view(*m) for m in group], (vrs, vrr, vts, vtr), z,
        lambda z_: dev(low, z_, c, hi, y), [at_g(*m) for m in group],
    )
    spread.start()
    drains.append(spread.drain)
    lane = lax.broadcasted_iota(jnp.int32, (8, 2048), 1)

    def key_positions(j, held):
        z_, c_, low_, h = j // 8, (j // 4) % 2, (j // 2) % 2, j % 2
        sid = spans[2 * (low_ * 16 + z_ * 2 + c_) + h]
        return jnp.where(lane // 32 == j, sid * 32 + lane % 32, held)

    kpos[...] = lax.fori_loop(
        0, 64, key_positions, jnp.zeros((8, 2048), jnp.int32)
    ).astype(F32)
    qring.forward(3)
    for g in (2, 3):
        norm_send(oc, g).wait_recv()
    spread.middle()
    oring.forward(1, otwin, (0,))
    oring.forward(1, otwin, (1,))
    if_keys(lambda: keys(1))
    qring.last()
    spread.last()
    accq[...] = jnp.zeros_like(accq)

    @pl.loop(0, 10)
    def _(i):
        part = rows_of(i * 512, 512, 512)
        accq[...] += jnp.dot(nb[:, part], wqb[part, :], preferred_element_type=F32)

    oring.forward(2, otwin, (0,))
    for i in range(4):
        rows = pl.ds(i * 128, 128)
        for h in range(2):
            qb[i, pl.ds(h * 128, 128), :] = head(
                accq[rows, pl.ds(h * 128, 128)], qg, rows
            ).astype(BF)
    pl.when(c == 1)(lambda: kv_wait(low, 0, 1))
    kv_wait(olow, 1, 1)
    spread.twins()

    scale = 128 ** (-0.5)

    def attend(c_, p):
        queries = qb[p * 2 + c_]
        scores = lax.dot_general(queries, kvp[0], NT, preferred_element_type=F32) * scale
        if p == 0:
            mine = rpos[rows_of(c_ * 128, 128, 128), :][:, :1]
            allowed = kpos[:1, :] <= jnp.concatenate([mine, mine], axis=0)
            scores = jnp.where(allowed, scores, -1e30)
        peak = jnp.max(scores, axis=-1, keepdims=True)
        if p == 1:
            own = lax.dot_general(queries, kvr[0], NT, preferred_element_type=F32) * scale
            q_row = lax.broadcasted_iota(jnp.int32, (256, 256), 0) % 128
            k_row = lax.broadcasted_iota(jnp.int32, (256, 256), 1)
            allowed = ((q_row // 64) == ((k_row // 64) % 2)) & (
                (k_row // 128) * 64 + k_row % 64 <= c_ * 64 + q_row % 64
            )
            own = jnp.where(allowed, own, -1e30)
            peak = jnp.maximum(peak, jnp.max(own, axis=-1, keepdims=True))
        weights = jnp.exp(scores - peak)
        total = jnp.sum(weights, axis=-1, keepdims=True)
        summed = jnp.dot(weights.astype(BF), kvp[1], preferred_element_type=F32)
        if p == 1:
            more = jnp.exp(own - peak)
            total = total + jnp.sum(more, axis=-1, keepdims=True)
            summed = summed + jnp.dot(more.astype(BF), kvr[1], preferred_element_type=F32)
        result = (summed / total).astype(BF)
        for h in range(2):
            atts[c_, pl.ds(p * 128, 128), pl.ds(h * 128, 128)] = result[h * 128 : (h + 1) * 128]

    def att_cols(low_, c_):
        return attb.at[:, rows_of((low_ * 2 + c_) * 256, 256, 256)]

    def att_send(i):
        low_, c_ = group[i]
        return remote(atts.at[c_], att_cols(low, c), ats.at[i], atr.at[i], at_g(low_, c_))

    oring.forward(2, otwin, (1,))
    attend(oc, 0)
    attend(oc, 1)
    att_send(2).start()
    att_send(0).start()
    attend(c, 0)
    attend(c, 1)
    att_send(1).start()
    oring.forward(3, otwin)
    drains.append(lambda: [att_send(i).wait_send() for i in range(3)])
    attb[:, rows_of((low * 2 + c) * 256, 256, 256)] = atts[c]
    other_own = wob.at[rows_of(z * 320 + oc * 160, 160, 32)]
    remote(other_own, other_own, o1.at[0], o1.at[1], twin).wait_recv()
    otwin.wait_recv(range(2))
    for i in range(3):
        part = att_cols(*group[i])
        remote(part, part, ats.at[i], atr.at[i], twin).wait_recv()

    early, late = (1 - z % 2) * 384, (z % 2) * 256

    def cols_of(k):
        return pl.ds(0, 640) if k < 3 else (
            rows_of(early, 256, 128) if k == 3 else rows_of(late, 384, 128)
        )

    def y_send(k, p, y_):
        place = (y_ - y + 3) % 4
        rows, cols = pl.ds(p * 128, 128), cols_of(k)
        return remote(
            osend.at[min(k, 3), rows, cols], ry.at[place, rows, cols],
            ys.at[k, p], yr.at[place, p, k // 4], at_y(y_),
        )

    def y_of(k):
        return (z // 2 + (0, 3 + 2 * (z % 2), 5 - 2 * (z % 2), 2, 2)[k]) % 4

    def project(k):
        y_ = y_of(k)
        first = y_ * 640 + (0, 0, 0, early, late)[k]
        weights = wob[rows_of(first, (640, 640, 640, 256, 384)[k], 128), :]
        osend[min(k, 3), :, cols_of(k)] = lax.dot_general(
            attb[...], weights, NT, preferred_element_type=F32
        ).astype(BF)
        for p in range(2):
            pl.when(y_ != y)(lambda p=p: y_send(k, p, y_).start())

    def drain_y():
        for k in range(5):
            for p in range(2):
                pl.when(y_of(k) != y)(lambda k=k, p=p: y_send(k, p, y_of(k)).wait_send())

    drains.append(drain_y)
    project(0)
    project(1)
    otwin.wait_recv((2,))
    project(2)
    project(3)
    oring.last(otwin)
    otwin.wait_recv((3,))
    project(4)

    def x_send(low_, p):
        return remote(
            xs.at[pl.ds(p * 128 + low_ * 64, 64)], xrx.at[hi, p],
            zs.at[low_, p], zr.at[hi, p], dev(low_, z, c, low, y),
        )

    mine = (y - z // 2 + 4) % 4
    slot = jnp.where(mine == 2, 3, jnp.where(mine % 2 == 0, 0, 2 - (mine // 2 + z) % 2))
    for p in range(2):
        rows = pl.ds(p * 128, 128)

        def y_wait(k, p=p):
            for i in range(3):
                part = ry.at[i, pl.ds(p * 128, 128), cols_of(k)]
                remote(part, part, ys.at[0, p], yr.at[i, p, k // 4], twin).wait_recv()

        @pl.when(mine == 2)
        def _(y_wait=y_wait):
            y_wait(3)
            y_wait(4)

        pl.when(mine != 2)(lambda: y_wait(0))
        total = osend[slot, rows, :].astype(F32)
        for i in range(3):
            total += ry[i, rows, :].astype(F32)
        xs[rows, :] = total.astype(BF)
        for low_ in range(2):
            here = jnp.logical_and(hi == low, low == low_)

            @pl.when(here)
            def _(low_=low_, p=p):
                xrx[hi, p] = xs[pl.ds(p * 128 + low_ * 64, 64), :]

            pl.when(jnp.logical_not(here))(lambda low_=low_, p=p: x_send(low_, p).start())

    offsets = c * 64 + lax.broadcasted_iota(jnp.int32, (64, 640), 0)
    for p in range(2):
        for hi_ in range(2):

            @pl.when(jnp.logical_not(jnp.logical_and(hi == low, hi == hi_)))
            def _(hi_=hi_, p=p):
                part = xrx.at[hi_, p]
                remote(part, part, zs.at[0, p], zr.at[hi_, p], twin).wait_recv()

        total = xrx[0, p].astype(F32) + xrx[1, p].astype(F32)
        if p == 0:
            both[pl.ds(0, 64), :] = total.astype(BF)
        else:
            both[pl.ds(64, 64), :] = jnp.where(offsets < lens[ctx // 2], total, 0.0).astype(BF)

    finish()
    for low_ in range(2):
        here = jnp.logical_and(hi == low, low == low_)

        @pl.when(jnp.logical_not(here))
        def _(low_=low_):
            for p in range(2):
                x_send(low_, p).wait_send()


def body(prompt_x, resp_x, span_ids, lengths, in_gain, q_gain, k_gain, w_query, w_keyval, w_out):
    half = 1000000.0 ** (-(np.arange(64) * 2.0) / 128)
    inverse = np.concatenate([half, half])[None, :].astype(np.float32)
    dma = pltpu.SemaphoreType.DMA
    hbm, vmem, smem = (pl.BlockSpec(memory_space=s) for s in (pl.ANY, pltpu.VMEM, pltpu.SMEM))
    out = jax.ShapeDtypeStruct((128, 640), BF)
    both = pl.pallas_call(
        kernel,
        out_shape=out,
        in_specs=[smem, smem, hbm, hbm, vmem, vmem, vmem, vmem, hbm, vmem, hbm],
        out_specs=vmem,
        scratch_shapes=[
            pltpu.VMEM((2, 128, 5120), BF),
            pltpu.VMEM((512, 5120), BF),
            pltpu.VMEM((5120, 256), BF),
            pltpu.VMEM((5120, 128), BF),
            pltpu.VMEM((2560, 1024), BF),
            pltpu.VMEM((2, 160, 128), BF),
            pltpu.VMEM((512, 256), F32),
            pltpu.VMEM((512, 128), F32),
            pltpu.VMEM((512, 128), F32),
            pltpu.VMEM((512, 128), F32),
            pltpu.VMEM((512, 128), F32),
            pltpu.VMEM((8, 2048), F32),
            pltpu.VMEM((4, 256, 128), BF),
            pltpu.VMEM((2, 2048, 128), BF),
            pltpu.VMEM((2, 256, 128), BF),
            pltpu.VMEM((2, 256, 256), BF),
            pltpu.VMEM((256, 1024), BF),
            pltpu.VMEM((4, 256, 640), BF),
            pltpu.VMEM((3, 256, 640), BF),
            pltpu.VMEM((256, 640), BF),
            pltpu.VMEM((2, 2, 64, 640), BF),
            dma((5,)),
            dma((2, 2, 2)), dma((2, 2, 2)),
            dma((2, 2, 2, 5)), dma((2, 2, 2, 5)),
            dma((3,)), dma((3,)),
            dma((3,)), dma((3,)),
            dma((2, 4, 4)), dma((2, 4, 4)),
            dma((2, 4, 4)), dma((2, 4, 4)),
            dma((2, 4, 2)), dma((2, 4, 2)),
            dma((2, 4, 2)), dma((2, 4, 2)),
            dma((2,)),
            dma((4,)), dma((4,)),
            dma((3, 2)), dma((2, 2)),
            dma((2, 4)), dma((2, 4)),
            dma((3, 2, 4)), dma((3, 2, 4)),
            dma((3,)), dma((3,)),
            dma((5, 2)), dma((3, 2, 2)),
            dma((2, 2)), dma((2, 2)),
        ],
        compiler_params=pltpu.CompilerParams(
            collective_id=0, has_side_effects=True, vmem_limit_bytes=56 * 2**20
        ),
        name="attention_block",
    )(
        span_ids, lengths, prompt_x, resp_x, in_gain[None, :], q_gain[None, :], k_gain[None, :],
        inverse, w_query, w_keyval, jnp.transpose(w_out),
    )
    return both[:64], both[64:]


def solution(mesh):
    placed = (
        P("ctx", "tp"),
        P("ctx", "tp"),
        P(),
        P(),
        P(),
        P(),
        P(),
        P("ctx", "tp"),
        P("ctx", None, "tp"),
        P("tp", "ctx"),
    )
    return jax.shard_map(
        body,
        mesh=mesh,
        in_specs=placed,
        out_specs=(P("ctx", "tp"), P("ctx", "tp")),
        check_vma=False,
    )
```
